32 devices in a mesh: pipe: 2 (over core), seq: 4 (over y, x), batch: 4 (over z).
Axes of the slice: x: 2, y: 2, z: 4, core: 2. Of those that a mesh axis runs over, the one named last changes fastest.
Arguments:
- latent: bfloat16 [32, 32, 2560], P('batch', 'seq'), parts along dimension 0, may hold values from -6 to 6
- w_qkv: bfloat16 [2, 2560, 3, 2560], P('pipe', None, None, 'seq')
- modulation: float32 [2, 8, 3, 2560], P('pipe'), may hold values from -3 to 3
- timestep: int32 [1], replicated, may hold values from 0 to 7
- order: int32 [32], P('batch'), parts along dimension 0, may hold values from 0 to 7, each once
- tiles: int32 [64, 6], P('batch'), parts along dimension 0, may hold values from 0 to 15, as said below
- stale_kv: bfloat16 [2, 32, 32, 2, 2560], P('pipe', 'batch', None, None, 'seq'), parts along dimension 1, may hold values from -6 to 6
Outputs:
- section_out: bfloat16 [2, 32, 32, 2560], P('pipe', 'batch', 'seq'), parts along dimension 1
The draws below stay inside these ranges and needn't reach their ends.
There are 4 independent parts, one for each index of `batch`. The reference program is written for one: setup_inputs(seed, part) draws one part's arguments, and reference() takes and returns one part's arrays. A program takes and returns all parts, laid end to end along the dimension named above; an argument that names none is the same for every part. Nothing has to cross between parts.
Inputs may be any that keep to these rules, and one draw needn't show every extreme that they name: Row g lists tile g first, then 6 - 1 distinct other tiles whose index differs from g modulo 16 by 1 to 5.
All inputs are finite; a program needn't handle non-finite values.
Results may differ from the reference program's by a relative error of at most 0.019.
Values may be sent and summed in bfloat16 or wider, within the bound.
A program may use at most 128 MiB of HBM per device.

```python
import jax
import jax.numpy as jnp
from jax import lax

D = 2560
HEADS = 20
HEAD_DIM = 128
STEPS = 8
PATCHES = 8
TILES_P = 2
NSEL = 6
SECTIONS = 2
PATCH_TOK = 32
TILE = 16
NTILES = 16


def draw_w_qkv(key, part):
    sampled = jax.random.normal(key, (SECTIONS, D, 3, D), jnp.float32) * D ** (-0.5)
    return sampled.astype(jnp.bfloat16)


def draw_tiles(key, part):
    window = 2 * (NSEL - 1)
    half_window = window // 2
    row_keys = jax.random.split(key, NTILES)
    picked = jax.vmap(lambda subkey: jax.random.permutation(subkey, window))(row_keys)[:, :NSEL - 1]
    offsets = jnp.where(picked < half_window, picked - half_window, picked - half_window + 1)
    anchor_tile = jnp.arange(NTILES, dtype=jnp.int32)[:, None]
    others = (anchor_tile + offsets) % NTILES
    return jnp.concatenate([anchor_tile, others.astype(jnp.int32)], axis=1).astype(jnp.int32)


def block_scale(rng, shape, cuts, smallest, top_value):
    loudness, own = 1.0, jax.random.fold_in(rng, 6)
    for dim, parts in cuts:
        draws = jnp.exp(jax.random.uniform(jax.random.fold_in(own, dim), (parts,), jnp.float32, smallest / len(cuts), top_value / len(cuts)))
        loudness = loudness * jnp.repeat(draws, shape[dim] // parts).reshape([-1 if axis == dim else 1 for axis in range(len(shape))])
    return loudness


def gaussian(stream_key, shape, deviation, limit, cuts=(), kind=jnp.bfloat16):
    drawn = deviation * jax.random.normal(stream_key, shape, jnp.float32)
    if cuts:
        drawn = drawn * block_scale(stream_key, shape, cuts, -0.22, 0.18)
    return jnp.clip(drawn, -limit, limit).astype(kind)


def setup_inputs(seed: int = 0, part: int = 0) -> dict:
    arg_keys = jax.random.split(jax.random.key(seed), 8)
    part_splits = jax.random.split(jax.random.fold_in(arg_keys[7], part), 8)
    return {
        "latent": gaussian(part_splits[0], (PATCHES, PATCH_TOK, D), 1.0, 6.0, ((1, 4),)),
        "w_qkv": draw_w_qkv(jax.random.fold_in(arg_keys[7], 71), part),
        "modulation": gaussian(arg_keys[2], (SECTIONS, STEPS, 3, D), 0.5, 3.0, ((0, 2),), jnp.float32),
        "timestep": jax.random.randint(arg_keys[3], (1,), 0, STEPS).astype(jnp.int32),
        "order": jax.random.permutation(part_splits[4], PATCHES).astype(jnp.int32),
        "tiles": draw_tiles(jax.random.fold_in(jax.random.fold_in(arg_keys[7], part), 71), part),
        "stale_kv": gaussian(part_splits[6], (SECTIONS, PATCHES, PATCH_TOK, 2, D), 1.0, 6.0, ((0, 2), (4, 4))),
    }


epsilon = 1e-06

def normalize(row_block, shift_row, scale_row):
    floated = row_block.astype(jnp.float32)
    average = lax.optimization_barrier(jnp.mean(floated, axis=-1, keepdims=True))
    centred = floated - average
    spread = lax.optimization_barrier(jnp.mean(centred * centred, axis=-1, keepdims=True))
    return (centred * lax.rsqrt(spread + epsilon) * (1.0 + scale_row) + shift_row).astype(jnp.bfloat16)

def attend(query, buffer, chosen_tiles):
    blocks = buffer.reshape(NTILES, TILE, 2, D)
    picked = blocks[chosen_tiles].reshape(TILES_P, NSEL * TILE, 2, HEADS, HEAD_DIM).astype(jnp.float32)
    queries = query.reshape(TILES_P, TILE, HEADS, HEAD_DIM).astype(jnp.float32)
    scores = jnp.einsum('qthd,qkhd->qhtk', queries, picked[:, :, 0]) * HEAD_DIM ** (-0.5)
    probabilities = jax.nn.softmax(scores, axis=-1).astype(jnp.bfloat16)
    mixed = jnp.einsum('qhtk,qkhd->qthd', probabilities.astype(jnp.float32), picked[:, :, 1])
    return mixed.reshape(PATCH_TOK, D).astype(jnp.bfloat16)

def reference(latent, w_qkv, modulation, timestep, order, tiles, stale_kv):
    hidden = latent
    section_outputs = []
    for section_id in range(SECTIONS):
        mod_row = modulation[section_id, timestep[0]]
        buffer = stale_kv[section_id]
        weights = w_qkv[section_id].reshape(D, 3 * D)
        updated = hidden
        for position in range(PATCHES):
            patch_id = order[position].astype(jnp.int32)
            own_rows = hidden[patch_id]
            normed = normalize(own_rows, mod_row[0], mod_row[1])
            projected = jnp.dot(normed, weights, preferred_element_type=jnp.float32).astype(jnp.bfloat16)
            projected = projected.reshape(PATCH_TOK, 3, D)
            buffer = buffer.at[patch_id].set(projected[:, 1:])
            chosen = lax.dynamic_slice_in_dim(tiles, (patch_id * TILES_P).astype(jnp.int32), TILES_P, 0)
            attended = attend(projected[:, 0], buffer, chosen)
            result = (own_rows.astype(jnp.float32) + mod_row[2] * attended.astype(jnp.float32)).astype(jnp.bfloat16)
            updated = updated.at[patch_id].set(result)
        hidden = updated
        section_outputs.append(hidden)
    return jnp.stack(section_outputs)
```

```python
import functools

import jax
import jax.numpy as jnp
from jax import lax
from jax.experimental import pallas as pl
from jax.experimental.pallas import tpu as pltpu
from jax.sharding import PartitionSpec as P

HEAD_DIM = 128
TILES_P = 2
EPSILON = 1e-06
MASKED = 1e30
MESH = pl.DeviceIdType.MESH
ROW_CHUNK = 16


def dot_t(a, b, dims):
    return lax.dot_general(a, b, (dims, ((), ())), preferred_element_type=jnp.float32)


def kernel(
    sizes,
    timestep_ref,
    order_ref,
    latent_ref,
    weights_ref,
    modulation_ref,
    tiles_ref,
    stale_ref,
    out_ref,
    hidden,
    normed,
    weights,
    stale,
    mods,
    bias,
    result,
    weight_sem,
    stale_sem,
    own_sem,
    lat_send,
    lat_recv,
    next_send,
    next_recv,
    out_send,
    out_recv,
    back_send,
    back_recv,
):
    patches, rows_dev, seq_count, pipe_count, heads = sizes
    stage = lax.axis_index("pipe")
    me = lax.axis_index("seq")
    last = pipe_count - 1
    block = patches * rows_dev
    tokens = block * seq_count
    local_w = heads * HEAD_DIM
    tile_len = rows_dev * seq_count // TILES_P
    ntiles = patches * TILES_P

    def rows_of(rank):
        return pl.ds(pl.multiple_of(rank * block, block), block)

    def columns_of(rank, head):
        return pl.ds(pl.multiple_of(rank * local_w + head * HEAD_DIM, HEAD_DIM), HEAD_DIM)

    def peer(step):
        return lax.rem(me + step, seq_count)

    def weight_copy(head, part):
        return pltpu.make_async_copy(
            weights_ref.at[part, :, pl.ds(head * HEAD_DIM, HEAD_DIM)],
            weights.at[head, :, pl.ds(part * HEAD_DIM, HEAD_DIM)],
            weight_sem.at[head, part],
        )

    def stale_copy():
        return pltpu.make_async_copy(stale_ref, stale, stale_sem)

    def own_latent():
        return pltpu.make_async_copy(latent_ref, hidden.at[rows_of(me)], own_sem)

    def latent_copy(step):
        return pltpu.make_async_remote_copy(
            src_ref=latent_ref,
            dst_ref=hidden.at[rows_of(me)],
            send_sem=lat_send.at[step],
            recv_sem=lat_recv.at[me],
            device_id={"seq": peer(step)},
            device_id_type=MESH,
        )

    def latent_arrival(source):
        return pltpu.make_async_remote_copy(
            src_ref=latent_ref,
            dst_ref=hidden.at[rows_of(source)],
            send_sem=lat_send.at[0],
            recv_sem=lat_recv.at[source],
            device_id={"seq": source},
            device_id_type=MESH,
        )

    def next_copy(head, step):
        return pltpu.make_async_remote_copy(
            src_ref=result.at[head],
            dst_ref=hidden.at[:, columns_of(me, head)],
            send_sem=next_send.at[head, step],
            recv_sem=next_recv.at[head, me],
            device_id={"pipe": stage + 1, "seq": peer(step)},
            device_id_type=MESH,
        )

    def next_arrival(head, source):
        return pltpu.make_async_remote_copy(
            src_ref=result.at[head],
            dst_ref=hidden.at[:, columns_of(source, head)],
            send_sem=next_send.at[head, 0],
            recv_sem=next_recv.at[head, source],
            device_id={"pipe": stage - 1, "seq": source},
            device_id_type=MESH,
        )

    def back_copy(target):
        return pltpu.make_async_remote_copy(
            src_ref=hidden.at[rows_of(me)],
            dst_ref=out_ref,
            send_sem=back_send,
            recv_sem=back_recv,
            device_id={"pipe": target},
            device_id_type=MESH,
        )

    def out_copy(head, step):
        return pltpu.make_async_remote_copy(
            src_ref=result.at[head, rows_of(peer(step))],
            dst_ref=out_ref.at[:, columns_of(me, head)],
            send_sem=out_send.at[head, step],
            recv_sem=out_recv.at[head, me],
            device_id={"seq": peer(step)},
            device_id_type=MESH,
        )

    def out_arrival(head, source):
        return pltpu.make_async_remote_copy(
            src_ref=result.at[head, rows_of(source)],
            dst_ref=out_ref.at[:, columns_of(source, head)],
            send_sem=out_send.at[head, 0],
            recv_sem=out_recv.at[head, source],
            device_id={"seq": source},
            device_id_type=MESH,
        )

    def out_own(head):
        return pltpu.make_async_copy(
            result.at[head, rows_of(me)],
            out_ref.at[:, columns_of(me, head)],
            out_send.at[head, 0],
        )

    barrier = pltpu.get_barrier_semaphore()
    for step in range(1, seq_count):
        pl.semaphore_signal(barrier, inc=1, device_id={"seq": peer(step)}, device_id_type=MESH)

    @pl.when(stage > 0)
    def _():
        for step in range(seq_count):
            pl.semaphore_signal(
                barrier, inc=1, device_id={"pipe": stage - 1, "seq": peer(step)}, device_id_type=MESH
            )

    @pl.when(stage < last)
    def _():
        for step in range(seq_count):
            pl.semaphore_signal(
                barrier, inc=1, device_id={"pipe": stage + 1, "seq": peer(step)}, device_id_type=MESH
            )

    @pl.when(stage == 0)
    def _():
        own_latent().start()

    for head in range(heads):
        for part in range(3):
            weight_copy(head, part).start()
    stale_copy().start()

    neighbours = (
        seq_count - 1
        + jnp.where(stage > 0, seq_count, 0)
        + jnp.where(stage < last, seq_count, 0)
    )
    pl.semaphore_wait(barrier, neighbours)

    @pl.when(stage == 0)
    def _():
        for step in range(1, seq_count):
            latent_copy(step).start()

    picked_step = lax.broadcasted_iota(jnp.int32, modulation_ref.shape[1:], 0) == timestep_ref[0]
    for part in range(3):
        row = jnp.sum(jnp.where(picked_step, modulation_ref[part], 0.0), axis=0, keepdims=True)
        mods[pl.ds(part, 1), :] = row + 1.0 if part == 1 else row

    key_tile = lax.broadcasted_iota(jnp.int32, (ntiles, ntiles), 0)
    query_tile = lax.broadcasted_iota(jnp.int32, (ntiles, ntiles), 1)
    chosen = jnp.zeros((ntiles, ntiles), jnp.float32)
    for j in range(tiles_ref.shape[0]):
        chosen = chosen + jnp.where(tiles_ref[pl.ds(j, 1), :] == key_tile, 1.0, 0.0)
    key_place = jnp.zeros((ntiles, ntiles), jnp.int32)
    query_place = jnp.zeros((ntiles, ntiles), jnp.int32)
    for t in range(patches):
        key_place = jnp.where(lax.div(key_tile, TILES_P) == order_ref[t], t, key_place)
        query_place = jnp.where(lax.div(query_tile, TILES_P) == order_ref[t], t, query_place)
    fresh = jnp.where(key_place <= query_place, chosen, 0.0)

    row_id = lax.broadcasted_iota(jnp.int32, (tokens, ntiles), 0)
    tile_id = lax.broadcasted_iota(jnp.int32, (tokens, ntiles), 1)
    in_block = lax.rem(row_id, block)
    token = lax.div(row_id, block) * rows_dev + lax.rem(in_block, rows_dev)
    tile_of_row = lax.div(in_block, rows_dev) * TILES_P + lax.div(token, tile_len)
    by_seq = jnp.where(tile_of_row == tile_id, 1.0, 0.0).astype(jnp.bfloat16)
    by_patch = jnp.where(lax.div(row_id, tile_len) == tile_id, 1.0, 0.0).astype(jnp.bfloat16)
    for place, (table, keys) in enumerate(((fresh, by_seq), (chosen - fresh, by_patch))):
        per_query = dot_t(by_seq, table.astype(jnp.bfloat16), ((1,), (1,)))
        seen = dot_t(per_query.astype(jnp.bfloat16), keys, ((1,), (1,)))
        bias[place] = (seen - 1.0) * MASKED

    @pl.when(stage > 0)
    def _():
        def arrive(head, carry):
            for source in range(seq_count):
                next_arrival(head, source).wait_recv()
            return carry

        lax.fori_loop(0, heads, arrive, 0)
        back_copy(stage - 1).start()

    def normalize_block(step, carry):
        source = peer(step)

        @pl.when((stage == 0) & (step == 0))
        def _():
            own_latent().wait()

        @pl.when((stage == 0) & (step > 0))
        def _():
            latent_arrival(source).wait_recv()

        def normalize_rows(part, inner):
            rows = pl.ds(pl.multiple_of(source * block + part * ROW_CHUNK, ROW_CHUNK), ROW_CHUNK)
            floated = hidden[rows, :].astype(jnp.float32)
            centred = floated - jnp.mean(floated, axis=-1, keepdims=True)
            spread = jnp.mean(centred * centred, axis=-1, keepdims=True)
            normed[rows, :] = (
                centred * lax.rsqrt(spread + EPSILON) * mods[1:2, :] + mods[0:1, :]
            ).astype(jnp.bfloat16)
            return inner

        return lax.fori_loop(0, block // ROW_CHUNK, normalize_rows, carry)

    lax.fori_loop(0, seq_count, normalize_block, 0)
    stale_copy().wait()

    def one_head(head, carry):
        for part in range(3):
            weight_copy(head, part).wait()
        projected = jnp.dot(
            normed[...], weights[head], preferred_element_type=jnp.float32
        ).astype(jnp.bfloat16)
        query = projected[:, :HEAD_DIM]
        key = projected[:, HEAD_DIM : 2 * HEAD_DIM]
        value = projected[:, 2 * HEAD_DIM :]
        lanes = pl.ds(pl.multiple_of(head * HEAD_DIM, HEAD_DIM), HEAD_DIM)
        scale = HEAD_DIM ** (-0.5)
        fresh_s = dot_t(query, key, ((1,), (1,))) * scale + bias[0]
        stale_s = dot_t(query, stale[0, :, lanes], ((1,), (1,))) * scale + bias[1]
        largest = jnp.maximum(
            jnp.max(fresh_s, axis=-1, keepdims=True), jnp.max(stale_s, axis=-1, keepdims=True)
        )
        fresh_p = jnp.exp(fresh_s - largest)
        stale_p = jnp.exp(stale_s - largest)
        total = jnp.sum(fresh_p, axis=-1, keepdims=True) + jnp.sum(stale_p, axis=-1, keepdims=True)
        mixed = jnp.dot(
            fresh_p.astype(jnp.bfloat16), value, preferred_element_type=jnp.float32
        ) + jnp.dot(
            stale_p.astype(jnp.bfloat16), stale[1, :, lanes], preferred_element_type=jnp.float32
        )
        attended = (mixed / total).astype(jnp.bfloat16).astype(jnp.float32)
        mine = columns_of(me, head)
        result[head] = (
            hidden[:, mine].astype(jnp.float32) + mods[2:3, mine] * attended
        ).astype(jnp.bfloat16)

        @pl.when(stage < last)
        def _():
            for step in range(seq_count):
                next_copy(head, step).start()

        @pl.when(stage == last)
        def _():
            for step in range(1, seq_count):
                out_copy(head, step).start()
            out_own(head).start()

        return carry

    lax.fori_loop(0, heads, one_head, 0)

    @pl.when(stage == 0)
    def _():
        for step in range(1, seq_count):
            latent_copy(step).wait_send()

    @pl.when(stage > 0)
    def _():
        back_copy(stage - 1).wait_send()

    @pl.when(stage < last)
    def _():
        def sent(head, carry):
            for step in range(seq_count):
                next_copy(head, step).wait_send()
            return carry

        lax.fori_loop(0, heads, sent, 0)
        back_copy(stage + 1).wait_recv()

    @pl.when(stage == last)
    def _():
        def done(head, carry):
            out_own(head).wait()
            for step in range(1, seq_count):
                out_copy(head, step).wait_send()
                out_arrival(head, peer(step)).wait_recv()
            return carry

        lax.fori_loop(0, heads, done, 0)


def local(latent, w_qkv, modulation, timestep, order, tiles, stale_kv):
    patches, rows_dev, width = latent.shape
    local_w = w_qkv.shape[3]
    heads = local_w // HEAD_DIM
    seq_count = lax.axis_size("seq")
    pipe_count = lax.axis_size("pipe")
    block = patches * rows_dev
    tokens = block * seq_count
    weights = jnp.transpose(w_qkv[0], (1, 0, 2))
    stale = jnp.transpose(stale_kv[0].reshape(tokens, 2, local_w), (1, 0, 2))
    mods = jnp.transpose(modulation[0], (1, 0, 2))
    smem = pl.BlockSpec(memory_space=pltpu.SMEM)
    vmem = pl.BlockSpec(memory_space=pltpu.VMEM)
    anywhere = pl.BlockSpec(memory_space=pl.ANY)
    bf16 = jnp.bfloat16
    dma = pltpu.SemaphoreType.DMA
    finished = pl.pallas_call(
        functools.partial(kernel, (patches, rows_dev, seq_count, pipe_count, heads)),
        out_shape=jax.ShapeDtypeStruct((block, width), bf16),
        in_specs=[smem, smem, anywhere, anywhere, vmem, vmem, anywhere],
        out_specs=anywhere,
        scratch_shapes=[
            pltpu.VMEM((tokens, width), bf16),
            pltpu.VMEM((tokens, width), bf16),
            pltpu.VMEM((heads, width, 3 * HEAD_DIM), bf16),
            pltpu.VMEM((2, tokens, local_w), bf16),
            pltpu.VMEM((8, width), jnp.float32),
            pltpu.VMEM((2, tokens, tokens), jnp.float32),
            pltpu.VMEM((heads, tokens, HEAD_DIM), bf16),
            dma((heads, 3)),
            dma(()),
            dma(()),
            dma((seq_count,)),
            dma((seq_count,)),
            dma((heads, seq_count)),
            dma((heads, seq_count)),
            dma((heads, seq_count)),
            dma((heads, seq_count)),
            dma(()),
            dma(()),
        ],
        compiler_params=pltpu.CompilerParams(
            collective_id=0, has_side_effects=True, vmem_limit_bytes=56 * 1024 * 1024
        ),
    )(timestep, order, latent.reshape(block, width), weights, mods, tiles.T, stale)
    return finished.reshape(1, patches, rows_dev, width)


def solution(mesh):
    return jax.shard_map(
        local,
        mesh=mesh,
        in_specs=(
            P("batch", "seq", None),
            P("pipe", None, None, "seq"),
            P("pipe", None, None, None),
            P(),
            P("batch"),
            P("batch", None),
            P("pipe", "batch", None, None, "seq"),
        ),
        out_specs=P("pipe", "batch", "seq", None),
        check_vma=False,
    )
```

```python
import functools

import jax
import jax.numpy as jnp
from jax import lax
from jax.experimental import pallas as pl
from jax.experimental.pallas import tpu as pltpu
from jax.sharding import PartitionSpec as P

HEAD_DIM = 128
TILES_P = 2
EPSILON = 1e-06
MASKED = 1e30
LOG2E = 1.4426950408889634
MESH = pl.DeviceIdType.MESH
ROW_CHUNK = 16


def dot_t(a, b, dims):
    return lax.dot_general(a, b, (dims, ((), ())), preferred_element_type=jnp.float32)


def kernel(
    sizes,
    timestep_ref,
    order_ref,
    latent_ref,
    weights_ref,
    modulation_ref,
    tiles_ref,
    stale_ref,
    out_ref,
    hidden,
    normed,
    weights,
    stale,
    mods,
    bias,
    result,
    qkv,
    weight_sem,
    stale_sem,
    own_sem,
    lat_send,
    lat_recv,
    next_send,
    next_recv,
    out_send,
    out_recv,
    back_send,
    back_recv,
):
    patches, rows_dev, seq_count, pipe_count, heads = sizes
    stage = lax.axis_index("pipe")
    me = lax.axis_index("seq")
    last = pipe_count - 1
    block = patches * rows_dev
    tokens = block * seq_count
    local_w = heads * HEAD_DIM
    tile_len = rows_dev * seq_count // TILES_P
    ntiles = patches * TILES_P

    def rows_of(rank):
        return pl.ds(pl.multiple_of(rank * block, block), block)

    def columns_of(rank, head):
        return pl.ds(pl.multiple_of(rank * local_w + head * HEAD_DIM, HEAD_DIM), HEAD_DIM)

    def peer(step):
        return lax.rem(me + step, seq_count)

    def weight_copy(head, part):
        return pltpu.make_async_copy(
            weights_ref.at[part, :, pl.ds(head * HEAD_DIM, HEAD_DIM)],
            weights.at[:, pl.ds((head * 3 + part) * HEAD_DIM, HEAD_DIM)],
            weight_sem.at[head, part],
        )

    def stale_copy():
        return pltpu.make_async_copy(stale_ref, stale, stale_sem)

    def own_latent():
        return pltpu.make_async_copy(latent_ref, hidden.at[rows_of(me)], own_sem)

    def latent_copy(step):
        return pltpu.make_async_remote_copy(
            src_ref=latent_ref,
            dst_ref=hidden.at[rows_of(me)],
            send_sem=lat_send.at[step],
            recv_sem=lat_recv.at[me],
            device_id={"seq": peer(step)},
            device_id_type=MESH,
        )

    def latent_arrival(source):
        return pltpu.make_async_remote_copy(
            src_ref=latent_ref,
            dst_ref=hidden.at[rows_of(source)],
            send_sem=lat_send.at[0],
            recv_sem=lat_recv.at[source],
            device_id={"seq": source},
            device_id_type=MESH,
        )

    def next_copy(head, step):
        return pltpu.make_async_remote_copy(
            src_ref=result.at[head],
            dst_ref=hidden.at[:, columns_of(me, head)],
            send_sem=next_send.at[head, step],
            recv_sem=next_recv.at[head, me],
            device_id={"pipe": stage + 1, "seq": peer(step)},
            device_id_type=MESH,
        )

    def next_arrival(head, source):
        return pltpu.make_async_remote_copy(
            src_ref=result.at[head],
            dst_ref=hidden.at[:, columns_of(source, head)],
            send_sem=next_send.at[head, 0],
            recv_sem=next_recv.at[head, source],
            device_id={"pipe": stage - 1, "seq": source},
            device_id_type=MESH,
        )

    def back_copy(target):
        return pltpu.make_async_remote_copy(
            src_ref=hidden.at[rows_of(me)],
            dst_ref=out_ref,
            send_sem=back_send,
            recv_sem=back_recv,
            device_id={"pipe": target},
            device_id_type=MESH,
        )

    def out_copy(head, step):
        return pltpu.make_async_remote_copy(
            src_ref=result.at[head, rows_of(peer(step))],
            dst_ref=out_ref.at[:, columns_of(me, head)],
            send_sem=out_send.at[head, step],
            recv_sem=out_recv.at[head, me],
            device_id={"seq": peer(step)},
            device_id_type=MESH,
        )

    def out_arrival(head, source):
        return pltpu.make_async_remote_copy(
            src_ref=result.at[head, rows_of(source)],
            dst_ref=out_ref.at[:, columns_of(source, head)],
            send_sem=out_send.at[head, 0],
            recv_sem=out_recv.at[head, source],
            device_id={"seq": source},
            device_id_type=MESH,
        )

    def out_own(head):
        return pltpu.make_async_copy(
            result.at[head, rows_of(me)],
            out_ref.at[:, columns_of(me, head)],
            out_send.at[head, 0],
        )

    barrier = pltpu.get_barrier_semaphore()
    for step in range(1, seq_count):
        pl.semaphore_signal(barrier, inc=1, device_id={"seq": peer(step)}, device_id_type=MESH)

    @pl.when(stage > 0)
    def _():
        for step in range(seq_count):
            pl.semaphore_signal(
                barrier, inc=1, device_id={"pipe": stage - 1, "seq": peer(step)}, device_id_type=MESH
            )

    @pl.when(stage < last)
    def _():
        for step in range(seq_count):
            pl.semaphore_signal(
                barrier, inc=1, device_id={"pipe": stage + 1, "seq": peer(step)}, device_id_type=MESH
            )

    @pl.when(stage == 0)
    def _():
        own_latent().start()

    for head in range(heads):
        for part in range(3):
            weight_copy(head, part).start()
    stale_copy().start()

    neighbours = (
        seq_count - 1
        + jnp.where(stage > 0, seq_count, 0)
        + jnp.where(stage < last, seq_count, 0)
    )
    pl.semaphore_wait(barrier, neighbours)

    @pl.when(stage == 0)
    def _():
        for step in range(1, seq_count):
            latent_copy(step).start()

    picked_step = lax.broadcasted_iota(jnp.int32, modulation_ref.shape[1:], 0) == timestep_ref[0]
    for part in range(3):
        row = jnp.sum(jnp.where(picked_step, modulation_ref[part], 0.0), axis=0, keepdims=True)
        mods[pl.ds(part, 1), :] = row + 1.0 if part == 1 else row

    key_tile = lax.broadcasted_iota(jnp.int32, (ntiles, ntiles), 0)
    query_tile = lax.broadcasted_iota(jnp.int32, (ntiles, ntiles), 1)
    chosen = jnp.zeros((ntiles, ntiles), jnp.float32)
    for j in range(tiles_ref.shape[0]):
        chosen = chosen + jnp.where(tiles_ref[pl.ds(j, 1), :] == key_tile, 1.0, 0.0)
    key_place = jnp.zeros((ntiles, ntiles), jnp.int32)
    query_place = jnp.zeros((ntiles, ntiles), jnp.int32)
    for t in range(patches):
        key_place = jnp.where(lax.div(key_tile, TILES_P) == order_ref[t], t, key_place)
        query_place = jnp.where(lax.div(query_tile, TILES_P) == order_ref[t], t, query_place)
    fresh = jnp.where(key_place <= query_place, chosen, 0.0)

    row_id = lax.broadcasted_iota(jnp.int32, (tokens, ntiles), 0)
    tile_id = lax.broadcasted_iota(jnp.int32, (tokens, ntiles), 1)
    in_block = lax.rem(row_id, block)
    token = lax.div(row_id, block) * rows_dev + lax.rem(in_block, rows_dev)
    tile_of_row = lax.div(in_block, rows_dev) * TILES_P + lax.div(token, tile_len)
    by_seq = jnp.where(tile_of_row == tile_id, 1.0, 0.0).astype(jnp.bfloat16)
    by_patch = jnp.where(lax.div(row_id, tile_len) == tile_id, 1.0, 0.0).astype(jnp.bfloat16)
    for place, (table, keys) in enumerate(((fresh, by_seq), (chosen - fresh, by_patch))):
        per_query = dot_t(by_seq, table.astype(jnp.bfloat16), ((1,), (1,)))
        seen = dot_t(per_query.astype(jnp.bfloat16), keys, ((1,), (1,)))
        bias[place] = (seen - 1.0) * MASKED

    @pl.when(stage > 0)
    def _():
        def arrive(head, carry):
            for source in range(seq_count):
                next_arrival(head, source).wait_recv()
            return carry

        lax.fori_loop(0, heads, arrive, 0)
        back_copy(stage - 1).start()

    def normalize_block(step, carry):
        source = peer(step)

        @pl.when((stage == 0) & (step == 0))
        def _():
            own_latent().wait()

        @pl.when((stage == 0) & (step > 0))
        def _():
            latent_arrival(source).wait_recv()

        def normalize_rows(part):
            rows = pl.ds(pl.multiple_of(source * block + part * ROW_CHUNK, ROW_CHUNK), ROW_CHUNK)
            floated = hidden[rows, :].astype(jnp.float32)
            centred = floated - jnp.mean(floated, axis=-1, keepdims=True)
            spread = jnp.mean(centred * centred, axis=-1, keepdims=True)
            normed[rows, :] = (
                centred * lax.rsqrt(spread + EPSILON) * mods[1:2, :] + mods[0:1, :]
            ).astype(jnp.bfloat16)

        for part in range(block // ROW_CHUNK):
            normalize_rows(part)
        return carry

    lax.fori_loop(0, seq_count, normalize_block, 0)
    stale_copy().wait()

    def project(group):
        for head in group:
            for part in range(3):
                weight_copy(head, part).wait()
        first, count = group[0], len(group)
        projected = jnp.dot(
            normed[...],
            weights[:, first * 3 * HEAD_DIM : (first + count) * 3 * HEAD_DIM],
            preferred_element_type=jnp.float32,
        )
        for place, head in enumerate(group):
            base = place * 3 * HEAD_DIM
            query = projected[:, base : base + HEAD_DIM] * (HEAD_DIM ** (-0.5) * LOG2E)
            qkv[head, 0] = query.astype(jnp.bfloat16)
            for part in (1, 2):
                piece = projected[:, base + part * HEAD_DIM : base + (part + 1) * HEAD_DIM]
                qkv[head, part] = piece.astype(jnp.bfloat16)

    def attend(head):
        query = qkv[head, 0]
        lanes = slice(head * HEAD_DIM, (head + 1) * HEAD_DIM)
        fresh_s = dot_t(query, qkv[head, 1], ((1,), (1,))) + bias[0]
        stale_s = dot_t(query, stale[0, :, lanes], ((1,), (1,))) + bias[1]
        largest = jnp.maximum(
            jnp.max(fresh_s, axis=-1, keepdims=True), jnp.max(stale_s, axis=-1, keepdims=True)
        )
        fresh_p = jnp.exp2(fresh_s - largest)
        stale_p = jnp.exp2(stale_s - largest)
        total = jnp.sum(fresh_p, axis=-1, keepdims=True) + jnp.sum(stale_p, axis=-1, keepdims=True)
        mixed = jnp.dot(
            fresh_p.astype(jnp.bfloat16), qkv[head, 2], preferred_element_type=jnp.float32
        ) + jnp.dot(
            stale_p.astype(jnp.bfloat16), stale[1, :, lanes], preferred_element_type=jnp.float32
        )
        attended = (mixed / total).astype(jnp.bfloat16).astype(jnp.float32)
        mine = columns_of(me, head)
        result[head] = (
            hidden[:, mine].astype(jnp.float32) + mods[2:3, mine] * attended
        ).astype(jnp.bfloat16)

    groups = [(0,)] + [
        tuple(range(head, min(head + 2, heads))) for head in range(1, heads, 2)
    ]
    project(groups[0])
    for place, group in enumerate(groups):
        if place + 1 < len(groups):
            project(groups[place + 1])
        for head in group:
            attend(head)

        @pl.when(stage < last)
        def _():
            for head in group:
                for step in range(seq_count):
                    next_copy(head, step).start()

        @pl.when(stage == last)
        def _():
            for head in group:
                for step in range(1, seq_count):
                    out_copy(head, step).start()
                out_own(head).start()

    @pl.when(stage == 0)
    def _():
        for step in range(1, seq_count):
            latent_copy(step).wait_send()

    @pl.when(stage > 0)
    def _():
        back_copy(stage - 1).wait_send()

    @pl.when(stage < last)
    def _():
        def sent(head, carry):
            for step in range(seq_count):
                next_copy(head, step).wait_send()
            return carry

        lax.fori_loop(0, heads, sent, 0)
        back_copy(stage + 1).wait_recv()

    @pl.when(stage == last)
    def _():
        def done(head, carry):
            out_own(head).wait()
            for step in range(1, seq_count):
                out_copy(head, step).wait_send()
                out_arrival(head, peer(step)).wait_recv()
            return carry

        lax.fori_loop(0, heads, done, 0)


def local(latent, w_qkv, modulation, timestep, order, tiles, stale_kv):
    patches, rows_dev, width = latent.shape
    local_w = w_qkv.shape[3]
    heads = local_w // HEAD_DIM
    seq_count = lax.axis_size("seq")
    pipe_count = lax.axis_size("pipe")
    block = patches * rows_dev
    tokens = block * seq_count
    weights = jnp.transpose(w_qkv[0], (1, 0, 2))
    stale = jnp.transpose(stale_kv[0].reshape(tokens, 2, local_w), (1, 0, 2))
    mods = jnp.transpose(modulation[0], (1, 0, 2))
    smem = pl.BlockSpec(memory_space=pltpu.SMEM)
    vmem = pl.BlockSpec(memory_space=pltpu.VMEM)
    anywhere = pl.BlockSpec(memory_space=pl.ANY)
    bf16 = jnp.bfloat16
    dma = pltpu.SemaphoreType.DMA
    finished = pl.pallas_call(
        functools.partial(kernel, (patches, rows_dev, seq_count, pipe_count, heads)),
        out_shape=jax.ShapeDtypeStruct((block, width), bf16),
        in_specs=[smem, smem, anywhere, anywhere, vmem, vmem, anywhere],
        out_specs=anywhere,
        scratch_shapes=[
            pltpu.VMEM((tokens, width), bf16),
            pltpu.VMEM((tokens, width), bf16),
            pltpu.VMEM((width, heads * 3 * HEAD_DIM), bf16),
            pltpu.VMEM((2, tokens, local_w), bf16),
            pltpu.VMEM((8, width), jnp.float32),
            pltpu.VMEM((2, tokens, tokens), jnp.float32),
            pltpu.VMEM((heads, tokens, HEAD_DIM), bf16),
            pltpu.VMEM((heads, 3, tokens, HEAD_DIM), bf16),
            dma((heads, 3)),
            dma(()),
            dma(()),
            dma((seq_count,)),
            dma((seq_count,)),
            dma((heads, seq_count)),
            dma((heads, seq_count)),
            dma((heads, seq_count)),
            dma((heads, seq_count)),
            dma(()),
            dma(()),
        ],
        compiler_params=pltpu.CompilerParams(
            collective_id=0, has_side_effects=True, vmem_limit_bytes=56 * 1024 * 1024
        ),
    )(timestep, order, latent.reshape(block, width), weights, mods, tiles.T, stale)
    return finished.reshape(1, patches, rows_dev, width)


def solution(mesh):
    return jax.shard_map(
        local,
        mesh=mesh,
        in_specs=(
            P("batch", "seq", None),
            P("pipe", None, None, "seq"),
            P("pipe", None, None, None),
            P(),
            P("batch"),
            P("batch", None),
            P("pipe", "batch", None, None, "seq"),
        ),
        out_specs=P("pipe", "batch", "seq", None),
        check_vma=False,
    )
```

```python
import functools

import jax
import jax.numpy as jnp
from jax import lax
from jax.experimental import pallas as pl
from jax.experimental.pallas import tpu as pltpu
from jax.sharding import PartitionSpec as P

HEAD_DIM = 128
TILES_P = 2
EPSILON = 1e-06
MASKED = 1e30
LOG2E = 1.4426950408889634
MESH = pl.DeviceIdType.MESH
ROW_CHUNK = 16


def dot_t(a, b, dims):
    return lax.dot_general(a, b, (dims, ((), ())), preferred_element_type=jnp.float32)


def kernel(
    sizes,
    timestep_ref,
    order_ref,
    latent_ref,
    weights_ref,
    modulation_ref,
    tiles_ref,
    stale_ref,
    out_ref,
    arrived,
    hidden,
    normed,
    weights,
    raw_stale,
    mixed_stale,
    stale,
    mods,
    bias,
    result,
    qkv,
    weight_sem,
    stale_sem,
    own_sem,
    lat_send,
    lat_recv,
    next_send,
    next_recv,
    out_send,
    out_recv,
    back_send,
    back_recv,
):
    patches, rows_dev, seq_count, pipe_count, heads = sizes
    stage = lax.axis_index("pipe")
    me = lax.axis_index("seq")
    last = pipe_count - 1
    block = patches * rows_dev
    tokens = block * seq_count
    local_w = heads * HEAD_DIM
    tile_len = rows_dev * seq_count // TILES_P
    ntiles = patches * TILES_P
    columns = seq_count * heads

    def rows_of(rank):
        return pl.ds(pl.multiple_of(rank * block, block), block)

    def columns_of(rank, head):
        return pl.ds(pl.multiple_of(rank * local_w + head * HEAD_DIM, HEAD_DIM), HEAD_DIM)

    def place_of(rank, head):
        return rank * heads + head

    def peer(step):
        return lax.rem(me + step, seq_count)

    def weight_copy(head, part):
        return pltpu.make_async_copy(
            weights_ref.at[part, :, pl.ds(head * HEAD_DIM, HEAD_DIM)],
            weights.at[:, pl.ds((head * 3 + part) * HEAD_DIM, HEAD_DIM)],
            weight_sem.at[head, part],
        )

    def stale_copy():
        return pltpu.make_async_copy(stale_ref, raw_stale, stale_sem)

    def own_latent():
        return pltpu.make_async_copy(latent_ref, arrived.at[rows_of(me)], own_sem)

    def latent_copy(step):
        return pltpu.make_async_remote_copy(
            src_ref=latent_ref,
            dst_ref=arrived.at[rows_of(me)],
            send_sem=lat_send.at[step],
            recv_sem=lat_recv.at[me],
            device_id={"seq": peer(step)},
            device_id_type=MESH,
        )

    def latent_arrival(source):
        return pltpu.make_async_remote_copy(
            src_ref=latent_ref,
            dst_ref=arrived.at[rows_of(source)],
            send_sem=lat_send.at[0],
            recv_sem=lat_recv.at[source],
            device_id={"seq": source},
            device_id_type=MESH,
        )

    def next_copy(head, step):
        return pltpu.make_async_remote_copy(
            src_ref=result.at[head],
            dst_ref=hidden.at[place_of(me, head)],
            send_sem=next_send.at[head, step],
            recv_sem=next_recv.at[head, me],
            device_id={"pipe": stage + 1, "seq": peer(step)},
            device_id_type=MESH,
        )

    def next_arrival(head, source):
        return pltpu.make_async_remote_copy(
            src_ref=result.at[head],
            dst_ref=hidden.at[place_of(source, head)],
            send_sem=next_send.at[head, 0],
            recv_sem=next_recv.at[head, source],
            device_id={"pipe": stage - 1, "seq": source},
            device_id_type=MESH,
        )

    def back_copy(target):
        return pltpu.make_async_remote_copy(
            src_ref=hidden.at[:, rows_of(me)],
            dst_ref=out_ref,
            send_sem=back_send,
            recv_sem=back_recv,
            device_id={"pipe": target},
            device_id_type=MESH,
        )

    def out_copy(head, step):
        return pltpu.make_async_remote_copy(
            src_ref=result.at[head, rows_of(peer(step))],
            dst_ref=out_ref.at[place_of(me, head)],
            send_sem=out_send.at[head, step],
            recv_sem=out_recv.at[head, me],
            device_id={"seq": peer(step)},
            device_id_type=MESH,
        )

    def out_arrival(head, source):
        return pltpu.make_async_remote_copy(
            src_ref=result.at[head, rows_of(source)],
            dst_ref=out_ref.at[place_of(source, head)],
            send_sem=out_send.at[head, 0],
            recv_sem=out_recv.at[head, source],
            device_id={"seq": source},
            device_id_type=MESH,
        )

    def out_own(head):
        return pltpu.make_async_copy(
            result.at[head, rows_of(me)],
            out_ref.at[place_of(me, head)],
            out_send.at[head, 0],
        )

    barrier = pltpu.get_barrier_semaphore()
    for step in range(1, seq_count):
        pl.semaphore_signal(barrier, inc=1, device_id={"seq": peer(step)}, device_id_type=MESH)

    @pl.when(stage > 0)
    def _():
        for step in range(seq_count):
            pl.semaphore_signal(
                barrier, inc=1, device_id={"pipe": stage - 1, "seq": peer(step)}, device_id_type=MESH
            )

    @pl.when(stage < last)
    def _():
        for step in range(seq_count):
            pl.semaphore_signal(
                barrier, inc=1, device_id={"pipe": stage + 1, "seq": peer(step)}, device_id_type=MESH
            )

    @pl.when(stage == 0)
    def _():
        own_latent().start()

    for head in range(heads):
        for part in range(3):
            weight_copy(head, part).start()
    stale_copy().start()

    neighbours = (
        seq_count - 1
        + jnp.where(stage > 0, seq_count, 0)
        + jnp.where(stage < last, seq_count, 0)
    )
    pl.semaphore_wait(barrier, neighbours)

    @pl.when(stage == 0)
    def _():
        for step in range(1, seq_count):
            latent_copy(step).start()

    picked_step = lax.broadcasted_iota(jnp.int32, modulation_ref.shape[1:], 0) == timestep_ref[0]
    for part in range(3):
        row = jnp.sum(jnp.where(picked_step, modulation_ref[part], 0.0), axis=0, keepdims=True)
        mods[pl.ds(part, 1), :] = row + 1.0 if part == 1 else row

    key_tile = lax.broadcasted_iota(jnp.int32, (ntiles, ntiles), 0)
    query_tile = lax.broadcasted_iota(jnp.int32, (ntiles, ntiles), 1)
    chosen = jnp.zeros((ntiles, ntiles), jnp.float32)
    for j in range(tiles_ref.shape[0]):
        chosen = chosen + jnp.where(tiles_ref[pl.ds(j, 1), :] == key_tile, 1.0, 0.0)
    key_place = jnp.zeros((ntiles, ntiles), jnp.int32)
    query_place = jnp.zeros((ntiles, ntiles), jnp.int32)
    for t in range(patches):
        key_place = jnp.where(lax.div(key_tile, TILES_P) == order_ref[t], t, key_place)
        query_place = jnp.where(lax.div(query_tile, TILES_P) == order_ref[t], t, query_place)
    fresh = jnp.where(key_place <= query_place, chosen, 0.0)

    row_id = lax.broadcasted_iota(jnp.int32, (tokens, ntiles), 0)
    tile_id = lax.broadcasted_iota(jnp.int32, (tokens, ntiles), 1)
    in_block = lax.rem(row_id, block)
    token = lax.div(row_id, block) * rows_dev + lax.rem(in_block, rows_dev)
    tile_of_row = lax.div(in_block, rows_dev) * TILES_P + lax.div(token, tile_len)
    by_seq = jnp.where(tile_of_row == tile_id, 1.0, 0.0).astype(jnp.bfloat16)
    by_patch = jnp.where(lax.div(row_id, tile_len) == tile_id, 1.0, 0.0).astype(jnp.bfloat16)
    for place, (table, keys) in enumerate(((fresh, by_seq), (chosen - fresh, by_patch))):
        per_query = dot_t(by_seq, table.astype(jnp.bfloat16), ((1,), (1,)))
        seen = dot_t(per_query.astype(jnp.bfloat16), keys, ((1,), (1,)))
        bias[place] = (seen - 1.0) * MASKED

    stale_copy().wait()
    mixed_stale[...] = raw_stale[...].reshape(2 * tokens, local_w)
    wanted = 2 * lax.broadcasted_iota(jnp.int32, (tokens, 2 * tokens), 0)
    present = lax.broadcasted_iota(jnp.int32, (tokens, 2 * tokens), 1)
    for part in range(2):
        select = jnp.where(wanted + part == present, 1.0, 0.0).astype(jnp.bfloat16)
        stale[part] = jnp.dot(
            select, mixed_stale[...], preferred_element_type=jnp.float32
        ).astype(jnp.bfloat16)

    @pl.when(stage > 0)
    def _():
        def arrive(head, carry):
            for source in range(seq_count):
                next_arrival(head, source).wait_recv()
            return carry

        lax.fori_loop(0, heads, arrive, 0)
        back_copy(stage - 1).start()

    def normalize_rows(rows, block_rows):
        floated = block_rows.astype(jnp.float32)
        centred = floated - jnp.mean(floated, axis=-1, keepdims=True)
        spread = jnp.mean(centred * centred, axis=-1, keepdims=True)
        normed[rows, :] = (
            centred * lax.rsqrt(spread + EPSILON) * mods[1:2, :] + mods[0:1, :]
        ).astype(jnp.bfloat16)

    def row_chunks(source):
        for part in range(block // ROW_CHUNK):
            yield pl.ds(pl.multiple_of(source * block + part * ROW_CHUNK, ROW_CHUNK), ROW_CHUNK)

    @pl.when(stage == 0)
    def _():
        own_latent().wait()

        def normalize_block(step, carry):
            source = peer(step)

            @pl.when(step > 0)
            def _():
                latent_arrival(source).wait_recv()

            for rows in row_chunks(source):
                block_rows = arrived[rows, :]
                normalize_rows(rows, block_rows)
                for place in range(columns):
                    hidden[place, rows, :] = block_rows[:, place * HEAD_DIM : (place + 1) * HEAD_DIM]
            return carry

        lax.fori_loop(0, seq_count, normalize_block, 0)

    @pl.when(stage > 0)
    def _():
        def normalize_block(source, carry):
            for rows in row_chunks(source):
                normalize_rows(
                    rows,
                    jnp.concatenate([hidden[place, rows, :] for place in range(columns)], axis=1),
                )
            return carry

        lax.fori_loop(0, seq_count, normalize_block, 0)

    def project(group):
        for head in group:
            for part in range(3):
                weight_copy(head, part).wait()
        first, count = group[0], len(group)
        projected = jnp.dot(
            normed[...],
            weights[:, first * 3 * HEAD_DIM : (first + count) * 3 * HEAD_DIM],
            preferred_element_type=jnp.float32,
        )
        for place, head in enumerate(group):
            base = place * 3 * HEAD_DIM
            query = projected[:, base : base + HEAD_DIM] * (HEAD_DIM ** (-0.5) * LOG2E)
            qkv[head, 0] = query.astype(jnp.bfloat16)
            for part in (1, 2):
                piece = projected[:, base + part * HEAD_DIM : base + (part + 1) * HEAD_DIM]
                qkv[head, part] = piece.astype(jnp.bfloat16)

    def attend(head):
        query = qkv[head, 0]
        lanes = slice(head * HEAD_DIM, (head + 1) * HEAD_DIM)
        fresh_s = dot_t(query, qkv[head, 1], ((1,), (1,))) + bias[0]
        stale_s = dot_t(query, stale[0, :, lanes], ((1,), (1,))) + bias[1]
        largest = jnp.maximum(
            jnp.max(fresh_s, axis=-1, keepdims=True), jnp.max(stale_s, axis=-1, keepdims=True)
        )
        fresh_p = jnp.exp2(fresh_s - largest)
        stale_p = jnp.exp2(stale_s - largest)
        total = jnp.sum(fresh_p, axis=-1, keepdims=True) + jnp.sum(stale_p, axis=-1, keepdims=True)
        mixed = jnp.dot(
            fresh_p.astype(jnp.bfloat16), qkv[head, 2], preferred_element_type=jnp.float32
        ) + jnp.dot(
            stale_p.astype(jnp.bfloat16), stale[1, :, lanes], preferred_element_type=jnp.float32
        )
        attended = (mixed / total).astype(jnp.bfloat16).astype(jnp.float32)
        mine = columns_of(me, head)
        result[head] = (
            hidden[place_of(me, head)].astype(jnp.float32) + mods[2:3, mine] * attended
        ).astype(jnp.bfloat16)

    groups = [(0,)] + [
        tuple(range(head, min(head + 2, heads))) for head in range(1, heads, 2)
    ]
    project(groups[0])
    for place, group in enumerate(groups):
        if place + 1 < len(groups):
            project(groups[place + 1])
        for head in group:
            attend(head)

        @pl.when(stage < last)
        def _():
            for head in group:
                for step in range(seq_count):
                    next_copy(head, step).start()

        @pl.when(stage == last)
        def _():
            for head in group:
                for step in range(1, seq_count):
                    out_copy(head, step).start()
                out_own(head).start()

    @pl.when(stage == 0)
    def _():
        for step in range(1, seq_count):
            latent_copy(step).wait_send()

    @pl.when(stage > 0)
    def _():
        back_copy(stage - 1).wait_send()

    @pl.when(stage < last)
    def _():
        def sent(head, carry):
            for step in range(seq_count):
                next_copy(head, step).wait_send()
            return carry

        lax.fori_loop(0, heads, sent, 0)
        back_copy(stage + 1).wait_recv()

    @pl.when(stage == last)
    def _():
        def done(head, carry):
            out_own(head).wait()
            for step in range(1, seq_count):
                out_copy(head, step).wait_send()
                out_arrival(head, peer(step)).wait_recv()
            return carry

        lax.fori_loop(0, heads, done, 0)


def local(latent, w_qkv, modulation, timestep, order, tiles, stale_kv):
    patches, rows_dev, width = latent.shape
    local_w = w_qkv.shape[3]
    heads = local_w // HEAD_DIM
    seq_count = lax.axis_size("seq")
    pipe_count = lax.axis_size("pipe")
    block = patches * rows_dev
    tokens = block * seq_count
    weights = jnp.transpose(w_qkv[0], (1, 0, 2))
    stale = stale_kv[0].reshape(tokens, 2, local_w)
    mods = jnp.transpose(modulation[0], (1, 0, 2))
    smem = pl.BlockSpec(memory_space=pltpu.SMEM)
    vmem = pl.BlockSpec(memory_space=pltpu.VMEM)
    anywhere = pl.BlockSpec(memory_space=pl.ANY)
    bf16 = jnp.bfloat16
    dma = pltpu.SemaphoreType.DMA
    finished = pl.pallas_call(
        functools.partial(kernel, (patches, rows_dev, seq_count, pipe_count, heads)),
        out_shape=jax.ShapeDtypeStruct((seq_count * heads, block, HEAD_DIM), bf16),
        in_specs=[smem, smem, anywhere, anywhere, vmem, vmem, anywhere],
        out_specs=anywhere,
        scratch_shapes=[
            pltpu.VMEM((tokens, width), bf16),
            pltpu.VMEM((seq_count * heads, tokens, HEAD_DIM), bf16),
            pltpu.VMEM((tokens, width), bf16),
            pltpu.VMEM((width, heads * 3 * HEAD_DIM), bf16),
            pltpu.VMEM((tokens, 2, local_w), bf16),
            pltpu.VMEM((2 * tokens, local_w), bf16),
            pltpu.VMEM((2, tokens, local_w), bf16),
            pltpu.VMEM((8, width), jnp.float32),
            pltpu.VMEM((2, tokens, tokens), jnp.float32),
            pltpu.VMEM((heads, tokens, HEAD_DIM), bf16),
            pltpu.VMEM((heads, 3, tokens, HEAD_DIM), bf16),
            dma((heads, 3)),
            dma(()),
            dma(()),
            dma((seq_count,)),
            dma((seq_count,)),
            dma((heads, seq_count)),
            dma((heads, seq_count)),
            dma((heads, seq_count)),
            dma((heads, seq_count)),
            dma(()),
            dma(()),
        ],
        compiler_params=pltpu.CompilerParams(
            collective_id=0, has_side_effects=True, vmem_limit_bytes=56 * 1024 * 1024
        ),
    )(timestep, order, latent.reshape(block, width), weights, mods, tiles.T, stale)
    return jnp.transpose(finished, (1, 0, 2)).reshape(1, patches, rows_dev, width)


def solution(mesh):
    return jax.shard_map(
        local,
        mesh=mesh,
        in_specs=(
            P("batch", "seq", None),
            P("pipe", None, None, "seq"),
            P("pipe", None, None, None),
            P(),
            P("batch"),
            P("batch", None),
            P("pipe", "batch", None, None, "seq"),
        ),
        out_specs=P("pipe", "batch", "seq", None),
        check_vma=False,
    )
```

```python
import functools

import jax
import jax.numpy as jnp
from jax import lax
from jax.experimental import pallas as pl
from jax.experimental.pallas import tpu as pltpu
from jax.sharding import PartitionSpec as P

HEAD_DIM = 128
TILES_P = 2
EPSILON = 1e-06
MASKED = 1e30
LOG2E = 1.4426950408889634
MESH = pl.DeviceIdType.MESH
ROW_CHUNK = 16


def dot_t(a, b, dims):
    return lax.dot_general(a, b, (dims, ((), ())), preferred_element_type=jnp.float32)


def kernel(
    sizes,
    timestep_ref,
    order_ref,
    latent_ref,
    weights_ref,
    modulation_ref,
    tiles_ref,
    stale_ref,
    out_ref,
    arrived,
    hidden,
    normed,
    weights,
    raw_stale,
    mixed_stale,
    stale,
    mods,
    bias,
    result,
    qkv,
    weight_sem,
    stale_sem,
    own_sem,
    lat_send,
    lat_recv,
    next_send,
    next_recv,
    out_send,
    out_recv,
    back_send,
    back_recv,
):
    patches, rows_dev, seq_count, pipe_count, heads = sizes
    stage = lax.axis_index("pipe")
    me = lax.axis_index("seq")
    last = pipe_count - 1
    block = patches * rows_dev
    tokens = block * seq_count
    local_w = heads * HEAD_DIM
    tile_len = rows_dev * seq_count // TILES_P
    ntiles = patches * TILES_P
    columns = seq_count * heads

    def rows_of(rank):
        return pl.ds(pl.multiple_of(rank * block, block), block)

    def columns_of(rank, head):
        return pl.ds(pl.multiple_of(rank * local_w + head * HEAD_DIM, HEAD_DIM), HEAD_DIM)

    def place_of(rank, head):
        return rank * heads + head

    def peer(step):
        return lax.rem(me + step, seq_count)

    def weight_copy(part):
        return pltpu.make_async_copy(weights_ref.at[part], weights.at[part], weight_sem.at[part])

    def stale_copy():
        return pltpu.make_async_copy(stale_ref, raw_stale, stale_sem)

    def own_latent():
        return pltpu.make_async_copy(latent_ref, arrived.at[rows_of(me)], own_sem)

    def latent_copy(step):
        return pltpu.make_async_remote_copy(
            src_ref=latent_ref,
            dst_ref=arrived.at[rows_of(me)],
            send_sem=lat_send.at[step],
            recv_sem=lat_recv.at[me],
            device_id={"seq": peer(step)},
            device_id_type=MESH,
        )

    def latent_arrival(source):
        return pltpu.make_async_remote_copy(
            src_ref=latent_ref,
            dst_ref=arrived.at[rows_of(source)],
            send_sem=lat_send.at[0],
            recv_sem=lat_recv.at[source],
            device_id={"seq": source},
            device_id_type=MESH,
        )

    def next_copy(head, step):
        return pltpu.make_async_remote_copy(
            src_ref=result.at[head],
            dst_ref=hidden.at[place_of(me, head)],
            send_sem=next_send.at[head, step],
            recv_sem=next_recv.at[head, me],
            device_id={"pipe": stage + 1, "seq": peer(step)},
            device_id_type=MESH,
        )

    def next_arrival(head, source):
        return pltpu.make_async_remote_copy(
            src_ref=result.at[head],
            dst_ref=hidden.at[place_of(source, head)],
            send_sem=next_send.at[head, 0],
            recv_sem=next_recv.at[head, source],
            device_id={"pipe": stage - 1, "seq": source},
            device_id_type=MESH,
        )

    def back_copy(target):
        return pltpu.make_async_remote_copy(
            src_ref=hidden.at[:, rows_of(me)],
            dst_ref=out_ref,
            send_sem=back_send,
            recv_sem=back_recv,
            device_id={"pipe": target},
            device_id_type=MESH,
        )

    def out_copy(head, step):
        return pltpu.make_async_remote_copy(
            src_ref=result.at[head, rows_of(peer(step))],
            dst_ref=out_ref.at[place_of(me, head)],
            send_sem=out_send.at[head, step],
            recv_sem=out_recv.at[head, me],
            device_id={"seq": peer(step)},
            device_id_type=MESH,
        )

    def out_arrival(head, source):
        return pltpu.make_async_remote_copy(
            src_ref=result.at[head, rows_of(source)],
            dst_ref=out_ref.at[place_of(source, head)],
            send_sem=out_send.at[head, 0],
            recv_sem=out_recv.at[head, source],
            device_id={"seq": source},
            device_id_type=MESH,
        )

    def out_own(head):
        return pltpu.make_async_copy(
            result.at[head, rows_of(me)],
            out_ref.at[place_of(me, head)],
            out_send.at[head, 0],
        )

    barrier = pltpu.get_barrier_semaphore()
    for step in range(1, seq_count):
        pl.semaphore_signal(barrier, inc=1, device_id={"seq": peer(step)}, device_id_type=MESH)

    @pl.when(stage > 0)
    def _():
        for step in range(seq_count):
            pl.semaphore_signal(
                barrier, inc=1, device_id={"pipe": stage - 1, "seq": peer(step)}, device_id_type=MESH
            )

    @pl.when(stage < last)
    def _():
        for step in range(seq_count):
            pl.semaphore_signal(
                barrier, inc=1, device_id={"pipe": stage + 1, "seq": peer(step)}, device_id_type=MESH
            )

    @pl.when(stage == 0)
    def _():
        own_latent().start()

    neighbours = (
        seq_count - 1
        + jnp.where(stage > 0, seq_count, 0)
        + jnp.where(stage < last, seq_count, 0)
    )
    pl.semaphore_wait(barrier, neighbours)

    @pl.when(stage == 0)
    def _():
        for step in range(1, seq_count):
            latent_copy(step).start()

    for part in range(3):
        weight_copy(part).start()
    stale_copy().start()

    picked_step = lax.broadcasted_iota(jnp.int32, modulation_ref.shape[1:], 0) == timestep_ref[0]
    for part in range(3):
        row = jnp.sum(jnp.where(picked_step, modulation_ref[part], 0.0), axis=0, keepdims=True)
        mods[pl.ds(part, 1), :] = row + 1.0 if part == 1 else row

    key_tile = lax.broadcasted_iota(jnp.int32, (ntiles, ntiles), 0)
    query_tile = lax.broadcasted_iota(jnp.int32, (ntiles, ntiles), 1)
    chosen = jnp.zeros((ntiles, ntiles), jnp.float32)
    for j in range(tiles_ref.shape[0]):
        chosen = chosen + jnp.where(tiles_ref[pl.ds(j, 1), :] == key_tile, 1.0, 0.0)
    key_place = jnp.zeros((ntiles, ntiles), jnp.int32)
    query_place = jnp.zeros((ntiles, ntiles), jnp.int32)
    for t in range(patches):
        key_place = jnp.where(lax.div(key_tile, TILES_P) == order_ref[t], t, key_place)
        query_place = jnp.where(lax.div(query_tile, TILES_P) == order_ref[t], t, query_place)
    fresh = jnp.where(key_place <= query_place, chosen, 0.0)

    row_id = lax.broadcasted_iota(jnp.int32, (tokens, ntiles), 0)
    tile_id = lax.broadcasted_iota(jnp.int32, (tokens, ntiles), 1)
    in_block = lax.rem(row_id, block)
    token = lax.div(row_id, block) * rows_dev + lax.rem(in_block, rows_dev)
    tile_of_row = lax.div(in_block, rows_dev) * TILES_P + lax.div(token, tile_len)
    by_seq = jnp.where(tile_of_row == tile_id, 1.0, 0.0).astype(jnp.bfloat16)
    by_patch = jnp.where(lax.div(row_id, tile_len) == tile_id, 1.0, 0.0).astype(jnp.bfloat16)
    for place, (table, keys) in enumerate(((fresh, by_seq), (chosen - fresh, by_patch))):
        per_query = dot_t(by_seq, table.astype(jnp.bfloat16), ((1,), (1,)))
        seen = dot_t(per_query.astype(jnp.bfloat16), keys, ((1,), (1,)))
        bias[place] = (seen - 1.0) * MASKED

    stale_copy().wait()
    mixed_stale[...] = raw_stale[...].reshape(2 * tokens, local_w)
    wanted = 2 * lax.broadcasted_iota(jnp.int32, (tokens, 2 * tokens), 0)
    present = lax.broadcasted_iota(jnp.int32, (tokens, 2 * tokens), 1)
    for part in range(2):
        select = jnp.where(wanted + part == present, 1.0, 0.0).astype(jnp.bfloat16)
        stale[part] = jnp.dot(
            select, mixed_stale[...], preferred_element_type=jnp.float32
        ).astype(jnp.bfloat16)

    @pl.when(stage > 0)
    def _():
        def arrive(head, carry):
            for source in range(seq_count):
                next_arrival(head, source).wait_recv()
            return carry

        lax.fori_loop(0, heads, arrive, 0)
        back_copy(stage - 1).start()

    def normalize_rows(rows, block_rows):
        floated = block_rows.astype(jnp.float32)
        centred = floated - jnp.mean(floated, axis=-1, keepdims=True)
        spread = jnp.mean(centred * centred, axis=-1, keepdims=True)
        normed[rows, :] = (
            centred * lax.rsqrt(spread + EPSILON) * mods[1:2, :] + mods[0:1, :]
        ).astype(jnp.bfloat16)

    def row_chunks(source):
        for part in range(block // ROW_CHUNK):
            yield pl.ds(pl.multiple_of(source * block + part * ROW_CHUNK, ROW_CHUNK), ROW_CHUNK)

    @pl.when(stage == 0)
    def _():
        own_latent().wait()

        def normalize_block(step, carry):
            source = peer(step)

            @pl.when(step > 0)
            def _():
                latent_arrival(source).wait_recv()

            for rows in row_chunks(source):
                block_rows = arrived[rows, :]
                normalize_rows(rows, block_rows)
                for place in range(columns):
                    hidden[place, rows, :] = block_rows[:, place * HEAD_DIM : (place + 1) * HEAD_DIM]
            return carry

        lax.fori_loop(0, seq_count, normalize_block, 0)

    @pl.when(stage > 0)
    def _():
        def normalize_block(source, carry):
            for rows in row_chunks(source):
                normalize_rows(
                    rows,
                    jnp.concatenate([hidden[place, rows, :] for place in range(columns)], axis=1),
                )
            return carry

        lax.fori_loop(0, seq_count, normalize_block, 0)

    for part in range(3):
        weight_copy(part).wait()

    def project(group):
        lanes = slice(group[0] * HEAD_DIM, (group[-1] + 1) * HEAD_DIM)
        span = len(group) * HEAD_DIM
        pieces = [weights[part, :, lanes] for part in range(3)]
        if len(group) == 1:
            pieces = [jnp.concatenate(pieces, axis=1)]
        projected = [
            jnp.dot(normed[...], piece, preferred_element_type=jnp.float32) for piece in pieces
        ]
        for part in range(3):
            whole = (
                projected[part]
                if len(projected) == 3
                else projected[0][:, part * span : (part + 1) * span]
            )
            if part == 0:
                whole = whole * (HEAD_DIM ** (-0.5) * LOG2E)
            for place, head in enumerate(group):
                qkv[head, part] = whole[:, place * HEAD_DIM : (place + 1) * HEAD_DIM].astype(
                    jnp.bfloat16
                )

    def attend(head):
        query = qkv[head, 0]
        lanes = slice(head * HEAD_DIM, (head + 1) * HEAD_DIM)
        fresh_s = dot_t(query, qkv[head, 1], ((1,), (1,))) + bias[0]
        stale_s = dot_t(query, stale[0, :, lanes], ((1,), (1,))) + bias[1]
        largest = jnp.maximum(
            jnp.max(fresh_s, axis=-1, keepdims=True), jnp.max(stale_s, axis=-1, keepdims=True)
        )
        fresh_p = jnp.exp2(fresh_s - largest)
        stale_p = jnp.exp2(stale_s - largest)
        total = jnp.sum(fresh_p, axis=-1, keepdims=True) + jnp.sum(stale_p, axis=-1, keepdims=True)
        mixed = jnp.dot(
            fresh_p.astype(jnp.bfloat16), qkv[head, 2], preferred_element_type=jnp.float32
        ) + jnp.dot(
            stale_p.astype(jnp.bfloat16), stale[1, :, lanes], preferred_element_type=jnp.float32
        )
        attended = (mixed / total).astype(jnp.bfloat16).astype(jnp.float32)
        mine = columns_of(me, head)
        result[head] = (
            hidden[place_of(me, head)].astype(jnp.float32) + mods[2:3, mine] * attended
        ).astype(jnp.bfloat16)

    groups = [(0,)] + [
        tuple(range(head, min(head + 2, heads))) for head in range(1, heads, 2)
    ]
    project(groups[0])
    for place, group in enumerate(groups):
        if place + 1 < len(groups):
            project(groups[place + 1])
        for head in group:
            attend(head)

        @pl.when(stage < last)
        def _():
            for head in group:
                for step in range(seq_count):
                    next_copy(head, step).start()

        @pl.when(stage == last)
        def _():
            for head in group:
                for step in range(1, seq_count):
                    out_copy(head, step).start()
                out_own(head).start()

    @pl.when(stage == 0)
    def _():
        for step in range(1, seq_count):
            latent_copy(step).wait_send()

    @pl.when(stage > 0)
    def _():
        back_copy(stage - 1).wait_send()

    @pl.when(stage < last)
    def _():
        def sent(head, carry):
            for step in range(seq_count):
                next_copy(head, step).wait_send()
            return carry

        lax.fori_loop(0, heads, sent, 0)
        back_copy(stage + 1).wait_recv()

    @pl.when(stage == last)
    def _():
        def done(head, carry):
            out_own(head).wait()
            for step in range(1, seq_count):
                out_copy(head, step).wait_send()
                out_arrival(head, peer(step)).wait_recv()
            return carry

        lax.fori_loop(0, heads, done, 0)


def local(latent, w_qkv, modulation, timestep, order, tiles, stale_kv):
    patches, rows_dev, width = latent.shape
    local_w = w_qkv.shape[3]
    heads = local_w // HEAD_DIM
    seq_count = lax.axis_size("seq")
    pipe_count = lax.axis_size("pipe")
    block = patches * rows_dev
    tokens = block * seq_count
    weights = jnp.transpose(w_qkv[0], (1, 0, 2))
    stale = stale_kv[0].reshape(tokens, 2, local_w)
    mods = jnp.transpose(modulation[0], (1, 0, 2))
    smem = pl.BlockSpec(memory_space=pltpu.SMEM)
    vmem = pl.BlockSpec(memory_space=pltpu.VMEM)
    anywhere = pl.BlockSpec(memory_space=pl.ANY)
    bf16 = jnp.bfloat16
    dma = pltpu.SemaphoreType.DMA
    finished = pl.pallas_call(
        functools.partial(kernel, (patches, rows_dev, seq_count, pipe_count, heads)),
        out_shape=jax.ShapeDtypeStruct((seq_count * heads, block, HEAD_DIM), bf16),
        in_specs=[smem, smem, anywhere, anywhere, vmem, vmem, anywhere],
        out_specs=anywhere,
        scratch_shapes=[
            pltpu.VMEM((tokens, width), bf16),
            pltpu.VMEM((seq_count * heads, tokens, HEAD_DIM), bf16),
            pltpu.VMEM((tokens, width), bf16),
            pltpu.VMEM((3, width, local_w), bf16),
            pltpu.VMEM((tokens, 2, local_w), bf16),
            pltpu.VMEM((2 * tokens, local_w), bf16),
            pltpu.VMEM((2, tokens, local_w), bf16),
            pltpu.VMEM((8, width), jnp.float32),
            pltpu.VMEM((2, tokens, tokens), jnp.float32),
            pltpu.VMEM((heads, tokens, HEAD_DIM), bf16),
            pltpu.VMEM((heads, 3, tokens, HEAD_DIM), bf16),
            dma((3,)),
            dma(()),
            dma(()),
            dma((seq_count,)),
            dma((seq_count,)),
            dma((heads, seq_count)),
            dma((heads, seq_count)),
            dma((heads, seq_count)),
            dma((heads, seq_count)),
            dma(()),
            dma(()),
        ],
        compiler_params=pltpu.CompilerParams(
            collective_id=0, has_side_effects=True, vmem_limit_bytes=56 * 1024 * 1024
        ),
    )(timestep, order, latent.reshape(block, width), weights, mods, tiles.T, stale)
    return jnp.transpose(finished, (1, 0, 2)).reshape(1, patches, rows_dev, width)


def solution(mesh):
    return jax.shard_map(
        local,
        mesh=mesh,
        in_specs=(
            P("batch", "seq", None),
            P("pipe", None, None, "seq"),
            P("pipe", None, None, None),
            P(),
            P("batch"),
            P("batch", None),
            P("pipe", "batch", None, None, "seq"),
        ),
        out_specs=P("pipe", "batch", "seq", None),
        check_vma=False,
    )
```

```python
import functools

import jax
import jax.numpy as jnp
from jax import lax
from jax.experimental import pallas as pl
from jax.experimental.pallas import tpu as pltpu
from jax.sharding import PartitionSpec as P

HEAD_DIM = 128
TILES_P = 2
EPSILON = 1e-06
MASKED = 1e30
LOG2E = 1.4426950408889634
MESH = pl.DeviceIdType.MESH
ROW_CHUNK = 16


def dot_t(a, b, dims):
    return lax.dot_general(a, b, (dims, ((), ())), preferred_element_type=jnp.float32)


def kernel(
    sizes,
    timestep_ref,
    order_ref,
    latent_ref,
    weights_ref,
    modulation_ref,
    tiles_ref,
    stale_ref,
    out_ref,
    arrived,
    hidden,
    normed,
    weights,
    raw_stale,
    mixed_stale,
    stale,
    mods,
    bias,
    result,
    qkv,
    weight_sem,
    stale_sem,
    own_sem,
    lat_send,
    lat_recv,
    next_send,
    next_recv,
    pass_send,
    out_send,
    out_recv,
    back_send,
    back_recv,
):
    patches, rows_dev, seq_count, pipe_count, heads = sizes
    stage = lax.axis_index("pipe")
    me = lax.axis_index("seq")
    last = pipe_count - 1
    block = patches * rows_dev
    tokens = block * seq_count
    local_w = heads * HEAD_DIM
    tile_len = rows_dev * seq_count // TILES_P
    ntiles = patches * TILES_P
    columns = seq_count * heads

    def rows_of(rank):
        return pl.ds(pl.multiple_of(rank * block, block), block)

    def columns_of(rank, head):
        return pl.ds(pl.multiple_of(rank * local_w + head * HEAD_DIM, HEAD_DIM), HEAD_DIM)

    def place_of(rank, head):
        return rank * heads + head

    square = 2
    across_x = lax.div(me, square) * square + (square - 1 - lax.rem(me, square))
    across_y = (square - 1 - lax.div(me, square)) * square + lax.rem(me, square)
    diagonal = seq_count - 1 - me

    def peer(step):
        return lax.rem(me + step, seq_count)

    def weight_copy(part):
        return pltpu.make_async_copy(weights_ref.at[part], weights.at[part], weight_sem.at[part])

    def stale_copy():
        return pltpu.make_async_copy(stale_ref, raw_stale, stale_sem)

    def own_latent():
        return pltpu.make_async_copy(latent_ref, arrived.at[rows_of(me)], own_sem)

    def half_of(rank, half, size):
        return pl.ds(pl.multiple_of(rank * size + half * (size // 2), size // 2), size // 2)

    def latent_copy(slot, half, target):
        return pltpu.make_async_remote_copy(
            src_ref=latent_ref.at[half_of(0, half, block)],
            dst_ref=arrived.at[half_of(me, half, block)],
            send_sem=lat_send.at[slot],
            recv_sem=lat_recv.at[me, half],
            device_id={"seq": target},
            device_id_type=MESH,
        )

    def latent_pass(slot, source, half, target):
        rows = half_of(source, half, block)
        return pltpu.make_async_remote_copy(
            src_ref=arrived.at[rows],
            dst_ref=arrived.at[rows],
            send_sem=lat_send.at[slot],
            recv_sem=lat_recv.at[source, half],
            device_id={"seq": target},
            device_id_type=MESH,
        )

    def latent_sends():
        return (
            latent_copy(0, 0, across_x),
            latent_copy(1, 1, across_y),
            latent_copy(2, 1, across_x),
            latent_copy(3, 0, across_y),
        )

    def latent_passes():
        return latent_pass(4, across_x, 0, across_y), latent_pass(5, across_y, 1, across_x)

    def next_copy(head, slot, half, target):
        rows = half_of(0, half, tokens)
        return pltpu.make_async_remote_copy(
            src_ref=result.at[head, rows],
            dst_ref=hidden.at[place_of(me, head), rows],
            send_sem=next_send.at[head, slot],
            recv_sem=next_recv.at[head, me, half],
            device_id={"pipe": stage + 1, "seq": target},
            device_id_type=MESH,
        )

    def next_sends(head):
        return (
            next_copy(head, 0, 0, across_x),
            next_copy(head, 1, 1, across_y),
            next_copy(head, 2, 1, across_x),
            next_copy(head, 3, 0, across_y),
            next_copy(head, 4, 0, me),
            next_copy(head, 5, 1, me),
        )

    def next_pass(head, slot, source, half, target):
        place = hidden.at[place_of(source, head), half_of(0, half, tokens)]
        return pltpu.make_async_remote_copy(
            src_ref=place,
            dst_ref=place,
            send_sem=pass_send.at[head, slot],
            recv_sem=next_recv.at[head, source, half],
            device_id={"seq": target},
            device_id_type=MESH,
        )

    def next_passes(head):
        return (
            next_pass(head, 0, across_x, 0, across_y),
            next_pass(head, 1, across_y, 1, across_x),
        )

    def back_copy(target):
        return pltpu.make_async_remote_copy(
            src_ref=hidden.at[:, rows_of(me)],
            dst_ref=out_ref,
            send_sem=back_send,
            recv_sem=back_recv,
            device_id={"pipe": target},
            device_id_type=MESH,
        )

    def out_copy(head, step):
        return pltpu.make_async_remote_copy(
            src_ref=result.at[head, rows_of(peer(step))],
            dst_ref=out_ref.at[place_of(me, head)],
            send_sem=out_send.at[head, step],
            recv_sem=out_recv.at[head, me],
            device_id={"seq": peer(step)},
            device_id_type=MESH,
        )

    def out_arrival(head, source):
        return pltpu.make_async_remote_copy(
            src_ref=result.at[head, rows_of(source)],
            dst_ref=out_ref.at[place_of(source, head)],
            send_sem=out_send.at[head, 0],
            recv_sem=out_recv.at[head, source],
            device_id={"seq": source},
            device_id_type=MESH,
        )

    def out_own(head):
        return pltpu.make_async_copy(
            result.at[head, rows_of(me)],
            out_ref.at[place_of(me, head)],
            out_send.at[head, 0],
        )

    barrier = pltpu.get_barrier_semaphore()
    for step in range(1, seq_count):
        pl.semaphore_signal(barrier, inc=1, device_id={"seq": peer(step)}, device_id_type=MESH)

    @pl.when(stage > 0)
    def _():
        for step in range(seq_count):
            pl.semaphore_signal(
                barrier, inc=1, device_id={"pipe": stage - 1, "seq": peer(step)}, device_id_type=MESH
            )

    @pl.when(stage < last)
    def _():
        for step in range(seq_count):
            pl.semaphore_signal(
                barrier, inc=1, device_id={"pipe": stage + 1, "seq": peer(step)}, device_id_type=MESH
            )

    @pl.when(stage == 0)
    def _():
        own_latent().start()

    neighbours = (
        seq_count - 1
        + jnp.where(stage > 0, seq_count, 0)
        + jnp.where(stage < last, seq_count, 0)
    )
    pl.semaphore_wait(barrier, neighbours)

    @pl.when(stage == 0)
    def _():
        for copy in latent_sends():
            copy.start()

    stale_copy().start()
    for part in range(3):
        weight_copy(part).start()

    picked_step = lax.broadcasted_iota(jnp.int32, modulation_ref.shape[1:], 0) == timestep_ref[0]
    for part in range(3):
        row = jnp.sum(jnp.where(picked_step, modulation_ref[part], 0.0), axis=0, keepdims=True)
        mods[pl.ds(part, 1), :] = row + 1.0 if part == 1 else row

    def normalize_rows(rows, block_rows):
        floated = block_rows.astype(jnp.float32)
        centred = floated - jnp.mean(floated, axis=-1, keepdims=True)
        spread = jnp.mean(centred * centred, axis=-1, keepdims=True)
        normed[rows, :] = (
            centred * lax.rsqrt(spread + EPSILON) * mods[1:2, :] + mods[0:1, :]
        ).astype(jnp.bfloat16)

    def row_chunks(source):
        for part in range(block // ROW_CHUNK):
            yield pl.ds(pl.multiple_of(source * block + part * ROW_CHUNK, ROW_CHUNK), ROW_CHUNK)

    def normalize_latent(source):
        for rows in row_chunks(source):
            block_rows = arrived[rows, :]
            normalize_rows(rows, block_rows)
            for place in range(columns):
                hidden[place, rows, :] = block_rows[:, place * HEAD_DIM : (place + 1) * HEAD_DIM]

    @pl.when(stage == 0)
    def _():
        own_latent().wait()
        normalize_latent(me)
        for source, half, copy in zip((across_x, across_y), (0, 1), latent_passes()):
            latent_pass(0, source, half, me).wait_recv()
            copy.start()

    key_tile = lax.broadcasted_iota(jnp.int32, (ntiles, ntiles), 0)
    query_tile = lax.broadcasted_iota(jnp.int32, (ntiles, ntiles), 1)
    chosen = jnp.zeros((ntiles, ntiles), jnp.float32)
    for j in range(tiles_ref.shape[0]):
        chosen = chosen + jnp.where(tiles_ref[pl.ds(j, 1), :] == key_tile, 1.0, 0.0)
    key_place = jnp.zeros((ntiles, ntiles), jnp.int32)
    query_place = jnp.zeros((ntiles, ntiles), jnp.int32)
    for t in range(patches):
        key_place = jnp.where(lax.div(key_tile, TILES_P) == order_ref[t], t, key_place)
        query_place = jnp.where(lax.div(query_tile, TILES_P) == order_ref[t], t, query_place)
    fresh = jnp.where(key_place <= query_place, chosen, 0.0)

    row_id = lax.broadcasted_iota(jnp.int32, (tokens, ntiles), 0)
    tile_id = lax.broadcasted_iota(jnp.int32, (tokens, ntiles), 1)
    in_block = lax.rem(row_id, block)
    token = lax.div(row_id, block) * rows_dev + lax.rem(in_block, rows_dev)
    tile_of_row = lax.div(in_block, rows_dev) * TILES_P + lax.div(token, tile_len)
    by_seq = jnp.where(tile_of_row == tile_id, 1.0, 0.0).astype(jnp.bfloat16)
    by_patch = jnp.where(lax.div(row_id, tile_len) == tile_id, 1.0, 0.0).astype(jnp.bfloat16)
    for place, (table, keys) in enumerate(((fresh, by_seq), (chosen - fresh, by_patch))):
        per_query = dot_t(by_seq, table.astype(jnp.bfloat16), ((1,), (1,)))
        seen = dot_t(per_query.astype(jnp.bfloat16), keys, ((1,), (1,)))
        bias[place] = (seen - 1.0) * MASKED

    stale_copy().wait()
    mixed_stale[...] = raw_stale[...].reshape(2 * tokens, local_w)
    wanted = 2 * lax.broadcasted_iota(jnp.int32, (tokens, 2 * tokens), 0)
    present = lax.broadcasted_iota(jnp.int32, (tokens, 2 * tokens), 1)
    for part in range(2):
        select = jnp.where(wanted + part == present, 1.0, 0.0).astype(jnp.bfloat16)
        stale[part] = jnp.dot(
            select, mixed_stale[...], preferred_element_type=jnp.float32
        ).astype(jnp.bfloat16)

    @pl.when(stage > 0)
    def _():
        def pass_on(head, carry):
            for source, half, copy in zip((across_x, across_y), (0, 1), next_passes(head)):
                next_pass(head, 0, source, half, across_x).wait_recv()
                copy.start()
            return carry

        def arrive(head, carry):
            for source, half in (
                (me, 0),
                (me, 1),
                (across_x, 1),
                (across_y, 0),
                (diagonal, 0),
                (diagonal, 1),
            ):
                next_pass(head, 0, source, half, across_x).wait_recv()
            return carry

        lax.fori_loop(0, heads, pass_on, 0)
        lax.fori_loop(0, heads, arrive, 0)
        back_copy(stage - 1).start()

    @pl.when(stage == 0)
    def _():
        latent_pass(0, across_x, 1, across_y).wait_recv()
        normalize_latent(across_x)
        latent_pass(0, across_y, 0, across_x).wait_recv()
        normalize_latent(across_y)
        latent_pass(0, diagonal, 0, across_x).wait_recv()
        latent_pass(0, diagonal, 1, across_x).wait_recv()
        normalize_latent(diagonal)

    @pl.when(stage > 0)
    def _():
        def normalize_block(source, carry):
            for rows in row_chunks(source):
                normalize_rows(
                    rows,
                    jnp.concatenate([hidden[place, rows, :] for place in range(columns)], axis=1),
                )
            return carry

        lax.fori_loop(0, seq_count, normalize_block, 0)

    for part in range(3):
        weight_copy(part).wait()

    def project(group):
        lanes = slice(group[0] * HEAD_DIM, (group[-1] + 1) * HEAD_DIM)
        span = len(group) * HEAD_DIM
        pieces = [weights[part, :, lanes] for part in range(3)]
        if len(group) == 1:
            pieces = [jnp.concatenate(pieces, axis=1)]
        projected = [
            jnp.dot(normed[...], piece, preferred_element_type=jnp.float32) for piece in pieces
        ]
        for part in range(3):
            whole = (
                projected[part]
                if len(projected) == 3
                else projected[0][:, part * span : (part + 1) * span]
            )
            if part == 0:
                whole = whole * (HEAD_DIM ** (-0.5) * LOG2E)
            for place, head in enumerate(group):
                qkv[head, part] = whole[:, place * HEAD_DIM : (place + 1) * HEAD_DIM].astype(
                    jnp.bfloat16
                )

    def attend(head):
        query = qkv[head, 0]
        lanes = slice(head * HEAD_DIM, (head + 1) * HEAD_DIM)
        fresh_s = dot_t(query, qkv[head, 1], ((1,), (1,))) + bias[0]
        stale_s = dot_t(query, stale[0, :, lanes], ((1,), (1,))) + bias[1]
        largest = jnp.maximum(
            jnp.max(fresh_s, axis=-1, keepdims=True), jnp.max(stale_s, axis=-1, keepdims=True)
        )
        fresh_p = jnp.exp2(fresh_s - largest)
        stale_p = jnp.exp2(stale_s - largest)
        total = jnp.sum(fresh_p, axis=-1, keepdims=True) + jnp.sum(stale_p, axis=-1, keepdims=True)
        mixed = jnp.dot(
            fresh_p.astype(jnp.bfloat16), qkv[head, 2], preferred_element_type=jnp.float32
        ) + jnp.dot(
            stale_p.astype(jnp.bfloat16), stale[1, :, lanes], preferred_element_type=jnp.float32
        )
        attended = (mixed / total).astype(jnp.bfloat16).astype(jnp.float32)
        mine = columns_of(me, head)
        result[head] = (
            hidden[place_of(me, head)].astype(jnp.float32) + mods[2:3, mine] * attended
        ).astype(jnp.bfloat16)

    groups = [(0,)] + [
        tuple(range(head, min(head + 2, heads))) for head in range(1, heads, 2)
    ]
    project(groups[0])
    for place, group in enumerate(groups):
        if place + 1 < len(groups):
            project(groups[place + 1])
        for head in group:
            attend(head)

        @pl.when(stage < last)
        def _():
            for head in group:
                for copy in next_sends(head):
                    copy.start()

        @pl.when(stage == last)
        def _():
            for head in group:
                for step in range(1, seq_count):
                    out_copy(head, step).start()
                out_own(head).start()

    @pl.when(stage == 0)
    def _():
        for copy in latent_sends() + latent_passes():
            copy.wait_send()

    @pl.when(stage > 0)
    def _():
        back_copy(stage - 1).wait_send()

        def passed(head, carry):
            for copy in next_passes(head):
                copy.wait_send()
            return carry

        lax.fori_loop(0, heads, passed, 0)

    @pl.when(stage < last)
    def _():
        def sent(head, carry):
            for copy in next_sends(head):
                copy.wait_send()
            return carry

        lax.fori_loop(0, heads, sent, 0)
        back_copy(stage + 1).wait_recv()

    @pl.when(stage == last)
    def _():
        def done(head, carry):
            out_own(head).wait()
            for step in range(1, seq_count):
                out_copy(head, step).wait_send()
                out_arrival(head, peer(step)).wait_recv()
            return carry

        lax.fori_loop(0, heads, done, 0)


def local(latent, w_qkv, modulation, timestep, order, tiles, stale_kv):
    patches, rows_dev, width = latent.shape
    local_w = w_qkv.shape[3]
    heads = local_w // HEAD_DIM
    seq_count = lax.axis_size("seq")
    pipe_count = lax.axis_size("pipe")
    block = patches * rows_dev
    tokens = block * seq_count
    weights = jnp.transpose(w_qkv[0], (1, 0, 2))
    stale = stale_kv[0].reshape(tokens, 2, local_w)
    mods = jnp.transpose(modulation[0], (1, 0, 2))
    smem = pl.BlockSpec(memory_space=pltpu.SMEM)
    vmem = pl.BlockSpec(memory_space=pltpu.VMEM)
    anywhere = pl.BlockSpec(memory_space=pl.ANY)
    bf16 = jnp.bfloat16
    dma = pltpu.SemaphoreType.DMA
    finished = pl.pallas_call(
        functools.partial(kernel, (patches, rows_dev, seq_count, pipe_count, heads)),
        out_shape=jax.ShapeDtypeStruct((seq_count * heads, block, HEAD_DIM), bf16),
        in_specs=[smem, smem, anywhere, anywhere, vmem, vmem, anywhere],
        out_specs=anywhere,
        scratch_shapes=[
            pltpu.VMEM((tokens, width), bf16),
            pltpu.VMEM((seq_count * heads, tokens, HEAD_DIM), bf16),
            pltpu.VMEM((tokens, width), bf16),
            pltpu.VMEM((3, width, local_w), bf16),
            pltpu.VMEM((tokens, 2, local_w), bf16),
            pltpu.VMEM((2 * tokens, local_w), bf16),
            pltpu.VMEM((2, tokens, local_w), bf16),
            pltpu.VMEM((8, width), jnp.float32),
            pltpu.VMEM((2, tokens, tokens), jnp.float32),
            pltpu.VMEM((heads, tokens, HEAD_DIM), bf16),
            pltpu.VMEM((heads, 3, tokens, HEAD_DIM), bf16),
            dma((3,)),
            dma(()),
            dma(()),
            dma((6,)),
            dma((seq_count, 2)),
            dma((heads, 6)),
            dma((heads, seq_count, 2)),
            dma((heads, 2)),
            dma((heads, seq_count)),
            dma((heads, seq_count)),
            dma(()),
            dma(()),
        ],
        compiler_params=pltpu.CompilerParams(
            collective_id=0, has_side_effects=True, vmem_limit_bytes=56 * 1024 * 1024
        ),
    )(timestep, order, latent.reshape(block, width), weights, mods, tiles.T, stale)
    return jnp.transpose(finished, (1, 0, 2)).reshape(1, patches, rows_dev, width)


def solution(mesh):
    return jax.shard_map(
        local,
        mesh=mesh,
        in_specs=(
            P("batch", "seq", None),
            P("pipe", None, None, "seq"),
            P("pipe", None, None, None),
            P(),
            P("batch"),
            P("batch", None),
            P("pipe", "batch", None, None, "seq"),
        ),
        out_specs=P("pipe", "batch", "seq", None),
        check_vma=False,
    )
```

```python
import functools

import jax
import jax.numpy as jnp
from jax import lax
from jax.experimental import pallas as pl
from jax.experimental.pallas import tpu as pltpu
from jax.sharding import PartitionSpec as P

HEAD_DIM = 128
TILES_P = 2
EPSILON = 1e-06
MASKED = 1e30
LOG2E = 1.4426950408889634
MESH = pl.DeviceIdType.MESH
ROW_CHUNK = 16


def dot_t(a, b, dims):
    return lax.dot_general(a, b, (dims, ((), ())), preferred_element_type=jnp.float32)


def kernel(
    sizes,
    timestep_ref,
    order_ref,
    latent_ref,
    weights_ref,
    modulation_ref,
    tiles_ref,
    stale_ref,
    out_ref,
    arrived,
    hidden,
    normed,
    weights,
    raw_stale,
    mixed_stale,
    stale,
    mods,
    bias,
    result,
    qkv,
    weight_sem,
    stale_sem,
    own_sem,
    lat_send,
    lat_recv,
    next_send,
    next_recv,
    pass_send,
    out_send,
    out_recv,
    back_send,
    back_recv,
):
    patches, rows_dev, seq_count, pipe_count, heads = sizes
    stage = lax.axis_index("pipe")
    me = lax.axis_index("seq")
    last = pipe_count - 1
    block = patches * rows_dev
    tokens = block * seq_count
    local_w = heads * HEAD_DIM
    tile_len = rows_dev * seq_count // TILES_P
    ntiles = patches * TILES_P
    columns = seq_count * heads

    def rows_of(rank):
        return pl.ds(pl.multiple_of(rank * block, block), block)

    def columns_of(rank, head):
        return pl.ds(pl.multiple_of(rank * local_w + head * HEAD_DIM, HEAD_DIM), HEAD_DIM)

    def place_of(rank, head):
        return rank * heads + head

    square = 2
    across_x = lax.div(me, square) * square + (square - 1 - lax.rem(me, square))
    across_y = (square - 1 - lax.div(me, square)) * square + lax.rem(me, square)
    diagonal = seq_count - 1 - me

    def peer(step):
        return lax.rem(me + step, seq_count)

    def weight_copy(part):
        return pltpu.make_async_copy(weights_ref.at[part], weights.at[part], weight_sem.at[part])

    def stale_copy():
        return pltpu.make_async_copy(stale_ref, raw_stale, stale_sem)

    def own_latent():
        return pltpu.make_async_copy(latent_ref, arrived.at[rows_of(me)], own_sem)

    def half_of(rank, half, size):
        return pl.ds(pl.multiple_of(rank * size + half * (size // 2), size // 2), size // 2)

    def latent_copy(slot, half, target):
        return pltpu.make_async_remote_copy(
            src_ref=latent_ref.at[half_of(0, half, block)],
            dst_ref=arrived.at[half_of(me, half, block)],
            send_sem=lat_send.at[slot],
            recv_sem=lat_recv.at[me, half],
            device_id={"seq": target},
            device_id_type=MESH,
        )

    def latent_pass(slot, source, half, target):
        rows = half_of(source, half, block)
        return pltpu.make_async_remote_copy(
            src_ref=arrived.at[rows],
            dst_ref=arrived.at[rows],
            send_sem=lat_send.at[slot],
            recv_sem=lat_recv.at[source, half],
            device_id={"seq": target},
            device_id_type=MESH,
        )

    def latent_sends():
        return (
            latent_copy(0, 0, across_x),
            latent_copy(1, 1, across_y),
            latent_copy(2, 1, across_x),
            latent_copy(3, 0, across_y),
        )

    def latent_passes():
        return latent_pass(4, across_x, 0, across_y), latent_pass(5, across_y, 1, across_x)

    def next_copy(head, slot, half, target):
        rows = half_of(0, half, tokens)
        return pltpu.make_async_remote_copy(
            src_ref=result.at[head, rows],
            dst_ref=hidden.at[place_of(me, head), rows],
            send_sem=next_send.at[head, slot],
            recv_sem=next_recv.at[head, me, half],
            device_id={"pipe": stage + 1, "seq": target},
            device_id_type=MESH,
        )

    def next_sends(head):
        return (
            next_copy(head, 0, 0, across_x),
            next_copy(head, 1, 1, across_y),
            next_copy(head, 2, 1, across_x),
            next_copy(head, 3, 0, across_y),
            next_copy(head, 4, 0, me),
            next_copy(head, 5, 1, me),
        )

    def next_pass(head, slot, source, half, target):
        place = hidden.at[place_of(source, head), half_of(0, half, tokens)]
        return pltpu.make_async_remote_copy(
            src_ref=place,
            dst_ref=place,
            send_sem=pass_send.at[head, slot],
            recv_sem=next_recv.at[head, source, half],
            device_id={"seq": target},
            device_id_type=MESH,
        )

    def next_passes(head):
        return (
            next_pass(head, 0, across_x, 0, across_y),
            next_pass(head, 1, across_y, 1, across_x),
        )

    def back_copy(place, target):
        return pltpu.make_async_remote_copy(
            src_ref=hidden.at[place, rows_of(me)],
            dst_ref=out_ref.at[:, columns_of(0, place)],
            send_sem=back_send.at[place],
            recv_sem=back_recv.at[place],
            device_id={"pipe": target},
            device_id_type=MESH,
        )

    def each_back(act):
        def one(place, carry):
            act(place)
            return carry

        lax.fori_loop(0, columns, one, 0)

    def out_copy(head, step):
        return pltpu.make_async_remote_copy(
            src_ref=result.at[head, rows_of(peer(step))],
            dst_ref=out_ref.at[:, columns_of(me, head)],
            send_sem=out_send.at[head, step],
            recv_sem=out_recv.at[head, me],
            device_id={"seq": peer(step)},
            device_id_type=MESH,
        )

    def out_arrival(head, source):
        return pltpu.make_async_remote_copy(
            src_ref=result.at[head, rows_of(source)],
            dst_ref=out_ref.at[:, columns_of(source, head)],
            send_sem=out_send.at[head, 0],
            recv_sem=out_recv.at[head, source],
            device_id={"seq": source},
            device_id_type=MESH,
        )

    def out_own(head):
        return pltpu.make_async_copy(
            result.at[head, rows_of(me)],
            out_ref.at[:, columns_of(me, head)],
            out_send.at[head, 0],
        )

    barrier = pltpu.get_barrier_semaphore()
    for step in range(1, seq_count):
        pl.semaphore_signal(barrier, inc=1, device_id={"seq": peer(step)}, device_id_type=MESH)

    @pl.when(stage > 0)
    def _():
        for step in range(seq_count):
            pl.semaphore_signal(
                barrier, inc=1, device_id={"pipe": stage - 1, "seq": peer(step)}, device_id_type=MESH
            )

    @pl.when(stage < last)
    def _():
        for step in range(seq_count):
            pl.semaphore_signal(
                barrier, inc=1, device_id={"pipe": stage + 1, "seq": peer(step)}, device_id_type=MESH
            )

    @pl.when(stage == 0)
    def _():
        own_latent().start()

    neighbours = (
        seq_count - 1
        + jnp.where(stage > 0, seq_count, 0)
        + jnp.where(stage < last, seq_count, 0)
    )
    pl.semaphore_wait(barrier, neighbours)

    @pl.when(stage == 0)
    def _():
        for copy in latent_sends():
            copy.start()

    stale_copy().start()
    for part in range(3):
        weight_copy(part).start()

    picked_step = lax.broadcasted_iota(jnp.int32, modulation_ref.shape[1:], 0) == timestep_ref[0]
    for part in range(3):
        row = jnp.sum(jnp.where(picked_step, modulation_ref[part], 0.0), axis=0, keepdims=True)
        mods[pl.ds(part, 1), :] = row + 1.0 if part == 1 else row

    def normalize_rows(rows, block_rows):
        floated = block_rows.astype(jnp.float32)
        centred = floated - jnp.mean(floated, axis=-1, keepdims=True)
        spread = jnp.mean(centred * centred, axis=-1, keepdims=True)
        normed[rows, :] = (
            centred * lax.rsqrt(spread + EPSILON) * mods[1:2, :] + mods[0:1, :]
        ).astype(jnp.bfloat16)

    def row_chunks(source):
        for part in range(block // ROW_CHUNK):
            yield pl.ds(pl.multiple_of(source * block + part * ROW_CHUNK, ROW_CHUNK), ROW_CHUNK)

    def normalize_latent(source):
        for rows in row_chunks(source):
            block_rows = arrived[rows, :]
            normalize_rows(rows, block_rows)
            for place in range(columns):
                hidden[place, rows, :] = block_rows[:, place * HEAD_DIM : (place + 1) * HEAD_DIM]

    @pl.when(stage == 0)
    def _():
        own_latent().wait()
        normalize_latent(me)
        for source, half, copy in zip((across_x, across_y), (0, 1), latent_passes()):
            latent_pass(0, source, half, me).wait_recv()
            copy.start()

    key_tile = lax.broadcasted_iota(jnp.int32, (ntiles, ntiles), 0)
    query_tile = lax.broadcasted_iota(jnp.int32, (ntiles, ntiles), 1)
    chosen = jnp.zeros((ntiles, ntiles), jnp.float32)
    for j in range(tiles_ref.shape[0]):
        chosen = chosen + jnp.where(tiles_ref[pl.ds(j, 1), :] == key_tile, 1.0, 0.0)
    key_place = jnp.zeros((ntiles, ntiles), jnp.int32)
    query_place = jnp.zeros((ntiles, ntiles), jnp.int32)
    for t in range(patches):
        key_place = jnp.where(lax.div(key_tile, TILES_P) == order_ref[t], t, key_place)
        query_place = jnp.where(lax.div(query_tile, TILES_P) == order_ref[t], t, query_place)
    fresh = jnp.where(key_place <= query_place, chosen, 0.0)

    row_id = lax.broadcasted_iota(jnp.int32, (tokens, ntiles), 0)
    tile_id = lax.broadcasted_iota(jnp.int32, (tokens, ntiles), 1)
    in_block = lax.rem(row_id, block)
    token = lax.div(row_id, block) * rows_dev + lax.rem(in_block, rows_dev)
    tile_of_row = lax.div(in_block, rows_dev) * TILES_P + lax.div(token, tile_len)
    by_seq = jnp.where(tile_of_row == tile_id, 1.0, 0.0).astype(jnp.bfloat16)
    by_patch = jnp.where(lax.div(row_id, tile_len) == tile_id, 1.0, 0.0).astype(jnp.bfloat16)
    for place, (table, keys) in enumerate(((fresh, by_seq), (chosen - fresh, by_patch))):
        per_query = dot_t(by_seq, table.astype(jnp.bfloat16), ((1,), (1,)))
        seen = dot_t(per_query.astype(jnp.bfloat16), keys, ((1,), (1,)))
        bias[place] = (seen - 1.0) * MASKED

    stale_copy().wait()
    mixed_stale[...] = raw_stale[...].reshape(2 * tokens, local_w)
    wanted = 2 * lax.broadcasted_iota(jnp.int32, (tokens, 2 * tokens), 0)
    present = lax.broadcasted_iota(jnp.int32, (tokens, 2 * tokens), 1)
    for part in range(2):
        select = jnp.where(wanted + part == present, 1.0, 0.0).astype(jnp.bfloat16)
        stale[part] = jnp.dot(
            select, mixed_stale[...], preferred_element_type=jnp.float32
        ).astype(jnp.bfloat16)

    @pl.when(stage > 0)
    def _():
        def pass_on(head, carry):
            for source, half, copy in zip((across_x, across_y), (0, 1), next_passes(head)):
                next_pass(head, 0, source, half, across_x).wait_recv()
                copy.start()
            return carry

        def arrive(head, carry):
            for source, half in (
                (me, 0),
                (me, 1),
                (across_x, 1),
                (across_y, 0),
                (diagonal, 0),
                (diagonal, 1),
            ):
                next_pass(head, 0, source, half, across_x).wait_recv()
            return carry

        lax.fori_loop(0, heads, pass_on, 0)
        lax.fori_loop(0, heads, arrive, 0)
        each_back(lambda place: back_copy(place, stage - 1).start())

    @pl.when(stage == 0)
    def _():
        latent_pass(0, across_x, 1, across_y).wait_recv()
        normalize_latent(across_x)
        latent_pass(0, across_y, 0, across_x).wait_recv()
        normalize_latent(across_y)
        latent_pass(0, diagonal, 0, across_x).wait_recv()
        latent_pass(0, diagonal, 1, across_x).wait_recv()
        normalize_latent(diagonal)

    @pl.when(stage > 0)
    def _():
        def normalize_block(source, carry):
            for rows in row_chunks(source):
                normalize_rows(
                    rows,
                    jnp.concatenate([hidden[place, rows, :] for place in range(columns)], axis=1),
                )
            return carry

        lax.fori_loop(0, seq_count, normalize_block, 0)

    for part in range(3):
        weight_copy(part).wait()

    def project(group):
        lanes = slice(group[0] * HEAD_DIM, (group[-1] + 1) * HEAD_DIM)
        span = len(group) * HEAD_DIM
        pieces = [weights[part, :, lanes] for part in range(3)]
        if len(group) == 1:
            pieces = [jnp.concatenate(pieces, axis=1)]
        projected = [
            jnp.dot(normed[...], piece, preferred_element_type=jnp.float32) for piece in pieces
        ]
        for part in range(3):
            whole = (
                projected[part]
                if len(projected) == 3
                else projected[0][:, part * span : (part + 1) * span]
            )
            if part == 0:
                whole = whole * (HEAD_DIM ** (-0.5) * LOG2E)
            for place, head in enumerate(group):
                qkv[head, part] = whole[:, place * HEAD_DIM : (place + 1) * HEAD_DIM].astype(
                    jnp.bfloat16
                )

    def attend(head):
        query = qkv[head, 0]
        lanes = slice(head * HEAD_DIM, (head + 1) * HEAD_DIM)
        fresh_s = dot_t(query, qkv[head, 1], ((1,), (1,))) + bias[0]
        stale_s = dot_t(query, stale[0, :, lanes], ((1,), (1,))) + bias[1]
        largest = jnp.maximum(
            jnp.max(fresh_s, axis=-1, keepdims=True), jnp.max(stale_s, axis=-1, keepdims=True)
        )
        fresh_p = jnp.exp2(fresh_s - largest)
        stale_p = jnp.exp2(stale_s - largest)
        ones = jnp.ones((tokens, HEAD_DIM), jnp.bfloat16)
        mixed = jnp.dot(
            fresh_p.astype(jnp.bfloat16),
            jnp.concatenate([qkv[head, 2], ones], axis=1),
            preferred_element_type=jnp.float32,
        ) + jnp.dot(
            stale_p.astype(jnp.bfloat16),
            jnp.concatenate([stale[1, :, lanes], ones], axis=1),
            preferred_element_type=jnp.float32,
        )
        attended = (mixed[:, :HEAD_DIM] / mixed[:, HEAD_DIM:]).astype(jnp.bfloat16).astype(jnp.float32)
        mine = columns_of(me, head)
        result[head] = (
            hidden[place_of(me, head)].astype(jnp.float32) + mods[2:3, mine] * attended
        ).astype(jnp.bfloat16)

    def send(head):
        @pl.when(stage < last)
        def _():
            for copy in next_sends(head):
                copy.start()

        @pl.when(stage == last)
        def _():
            for step in range(1, seq_count):
                out_copy(head, step).start()
            out_own(head).start()

    groups = [(0,)] + [
        tuple(range(head, min(head + 2, heads))) for head in range(1, heads, 2)
    ]
    project(groups[0])
    attend(0)
    send(0)
    if heads > 1:
        project(groups[1])
    for place, group in enumerate(groups[1:], 1):
        for head in group:
            if head == group[-1] and place + 1 < len(groups):
                project(groups[place + 1])
            attend(head)
            send(head)

    @pl.when(stage == 0)
    def _():
        for copy in latent_sends() + latent_passes():
            copy.wait_send()

    @pl.when(stage > 0)
    def _():
        each_back(lambda place: back_copy(place, stage - 1).wait_send())

        def passed(head, carry):
            for copy in next_passes(head):
                copy.wait_send()
            return carry

        lax.fori_loop(0, heads, passed, 0)

    @pl.when(stage < last)
    def _():
        def sent(head, carry):
            for copy in next_sends(head):
                copy.wait_send()
            return carry

        lax.fori_loop(0, heads, sent, 0)
        each_back(lambda place: back_copy(place, stage + 1).wait_recv())

    @pl.when(stage == last)
    def _():
        def done(head, carry):
            out_own(head).wait()
            for step in range(1, seq_count):
                out_copy(head, step).wait_send()
                out_arrival(head, peer(step)).wait_recv()
            return carry

        lax.fori_loop(0, heads, done, 0)


def local(latent, w_qkv, modulation, timestep, order, tiles, stale_kv):
    patches, rows_dev, width = latent.shape
    local_w = w_qkv.shape[3]
    heads = local_w // HEAD_DIM
    seq_count = lax.axis_size("seq")
    pipe_count = lax.axis_size("pipe")
    block = patches * rows_dev
    tokens = block * seq_count
    weights = jnp.transpose(w_qkv[0], (1, 0, 2))
    stale = stale_kv[0].reshape(tokens, 2, local_w)
    mods = jnp.transpose(modulation[0], (1, 0, 2))
    smem = pl.BlockSpec(memory_space=pltpu.SMEM)
    vmem = pl.BlockSpec(memory_space=pltpu.VMEM)
    anywhere = pl.BlockSpec(memory_space=pl.ANY)
    bf16 = jnp.bfloat16
    dma = pltpu.SemaphoreType.DMA
    finished = pl.pallas_call(
        functools.partial(kernel, (patches, rows_dev, seq_count, pipe_count, heads)),
        out_shape=jax.ShapeDtypeStruct((block, width), bf16),
        in_specs=[smem, smem, anywhere, anywhere, vmem, vmem, anywhere],
        out_specs=anywhere,
        scratch_shapes=[
            pltpu.VMEM((tokens, width), bf16),
            pltpu.VMEM((seq_count * heads, tokens, HEAD_DIM), bf16),
            pltpu.VMEM((tokens, width), bf16),
            pltpu.VMEM((3, width, local_w), bf16),
            pltpu.VMEM((tokens, 2, local_w), bf16),
            pltpu.VMEM((2 * tokens, local_w), bf16),
            pltpu.VMEM((2, tokens, local_w), bf16),
            pltpu.VMEM((8, width), jnp.float32),
            pltpu.VMEM((2, tokens, tokens), jnp.float32),
            pltpu.VMEM((heads, tokens, HEAD_DIM), bf16),
            pltpu.VMEM((heads, 3, tokens, HEAD_DIM), bf16),
            dma((3,)),
            dma(()),
            dma(()),
            dma((6,)),
            dma((seq_count, 2)),
            dma((heads, 6)),
            dma((heads, seq_count, 2)),
            dma((heads, 2)),
            dma((heads, seq_count)),
            dma((heads, seq_count)),
            dma((seq_count * heads,)),
            dma((seq_count * heads,)),
        ],
        compiler_params=pltpu.CompilerParams(
            collective_id=0, has_side_effects=True, vmem_limit_bytes=56 * 1024 * 1024
        ),
    )(timestep, order, latent.reshape(block, width), weights, mods, tiles.T, stale)
    return finished.reshape(1, patches, rows_dev, width)


def solution(mesh):
    return jax.shard_map(
        local,
        mesh=mesh,
        in_specs=(
            P("batch", "seq", None),
            P("pipe", None, None, "seq"),
            P("pipe", None, None, None),
            P(),
            P("batch"),
            P("batch", None),
            P("pipe", "batch", None, None, "seq"),
        ),
        out_specs=P("pipe", "batch", "seq", None),
        check_vma=False,
    )
```

```python
import functools

import jax
import jax.numpy as jnp
from jax import lax
from jax.experimental import pallas as pl
from jax.experimental.pallas import tpu as pltpu
from jax.sharding import PartitionSpec as P

HEAD_DIM = 128
TILES_P = 2
EPSILON = 1e-06
MASKED = 1e30
LOG2E = 1.4426950408889634
MESH = pl.DeviceIdType.MESH
ROW_CHUNK = 16


def dot_t(a, b, dims):
    return lax.dot_general(a, b, (dims, ((), ())), preferred_element_type=jnp.float32)


def kernel(
    sizes,
    timestep_ref,
    order_ref,
    latent_ref,
    weights_ref,
    modulation_ref,
    tiles_ref,
    stale_ref,
    out_ref,
    arrived,
    hidden,
    normed,
    weights,
    raw_stale,
    mixed_stale,
    stale,
    mods,
    bias,
    result,
    qkv,
    weight_sem,
    stale_sem,
    own_sem,
    lat_send,
    lat_recv,
    next_send,
    next_recv,
    pass_send,
    out_send,
    out_recv,
    back_send,
    back_recv,
):
    patches, rows_dev, seq_count, pipe_count, heads = sizes
    stage = lax.axis_index("pipe")
    me = lax.axis_index("seq")
    last = pipe_count - 1
    helper = min(1, last)
    block = patches * rows_dev
    tokens = block * seq_count
    local_w = heads * HEAD_DIM
    tile_len = rows_dev * seq_count // TILES_P
    ntiles = patches * TILES_P
    columns = seq_count * heads

    def rows_of(rank):
        return pl.ds(pl.multiple_of(rank * block, block), block)

    def columns_of(rank, head):
        return pl.ds(pl.multiple_of(rank * local_w + head * HEAD_DIM, HEAD_DIM), HEAD_DIM)

    def place_of(rank, head):
        return rank * heads + head

    square = 2
    across_x = lax.div(me, square) * square + (square - 1 - lax.rem(me, square))
    across_y = (square - 1 - lax.div(me, square)) * square + lax.rem(me, square)
    diagonal = seq_count - 1 - me

    def peer(step):
        return lax.rem(me + step, seq_count)

    def weight_copy(part):
        return pltpu.make_async_copy(weights_ref.at[part], weights.at[part], weight_sem.at[part])

    def stale_copy():
        return pltpu.make_async_copy(stale_ref, raw_stale, stale_sem)

    def own_latent():
        return pltpu.make_async_copy(latent_ref, arrived.at[rows_of(me)], own_sem)

    def half_of(rank, half, size):
        return pl.ds(pl.multiple_of(rank * size + half * (size // 2), size // 2), size // 2)

    def latent_copy(slot, half, target):
        return pltpu.make_async_remote_copy(
            src_ref=latent_ref.at[half_of(0, half, block)],
            dst_ref=arrived.at[half_of(me, half, block)],
            send_sem=lat_send.at[slot],
            recv_sem=lat_recv.at[me, half],
            device_id={"pipe": 0, "seq": target},
            device_id_type=MESH,
        )

    def latent_pass(slot, source, half, target):
        rows = half_of(source, half, block)
        return pltpu.make_async_remote_copy(
            src_ref=arrived.at[rows],
            dst_ref=arrived.at[rows],
            send_sem=lat_send.at[slot],
            recv_sem=lat_recv.at[source, half],
            device_id={"seq": target},
            device_id_type=MESH,
        )

    def latent_sends_x():
        return latent_copy(0, 0, across_x), latent_copy(2, 1, across_x)

    def latent_sends_y():
        return latent_copy(1, 1, across_y), latent_copy(3, 0, across_y)

    def latent_passes():
        return latent_pass(4, across_x, 0, across_y), latent_pass(5, across_y, 1, across_x)

    def next_copy(head, slot, half, target):
        rows = half_of(0, half, tokens)
        return pltpu.make_async_remote_copy(
            src_ref=result.at[head, rows],
            dst_ref=hidden.at[place_of(me, head), rows],
            send_sem=next_send.at[head, slot],
            recv_sem=next_recv.at[head, me, half],
            device_id={"pipe": stage + 1, "seq": target},
            device_id_type=MESH,
        )

    def next_sends(head):
        return (
            next_copy(head, 0, 0, across_x),
            next_copy(head, 1, 1, across_y),
            next_copy(head, 2, 1, across_x),
            next_copy(head, 3, 0, across_y),
            next_copy(head, 4, 0, me),
            next_copy(head, 5, 1, me),
        )

    def next_pass(head, slot, source, half, target):
        place = hidden.at[place_of(source, head), half_of(0, half, tokens)]
        return pltpu.make_async_remote_copy(
            src_ref=place,
            dst_ref=place,
            send_sem=pass_send.at[head, slot],
            recv_sem=next_recv.at[head, source, half],
            device_id={"seq": target},
            device_id_type=MESH,
        )

    def next_passes(head):
        return (
            next_pass(head, 0, across_x, 0, across_y),
            next_pass(head, 1, across_y, 1, across_x),
        )

    def back_copy(place, target):
        return pltpu.make_async_remote_copy(
            src_ref=hidden.at[place, rows_of(me)],
            dst_ref=out_ref.at[:, columns_of(0, place)],
            send_sem=back_send.at[place],
            recv_sem=back_recv.at[place],
            device_id={"pipe": target},
            device_id_type=MESH,
        )

    def each_back(act):
        def one(place, carry):
            act(place)
            return carry

        lax.fori_loop(0, columns, one, 0)

    def out_copy(head, step):
        return pltpu.make_async_remote_copy(
            src_ref=result.at[head, rows_of(peer(step))],
            dst_ref=out_ref.at[:, columns_of(me, head)],
            send_sem=out_send.at[head, step],
            recv_sem=out_recv.at[head, me],
            device_id={"seq": peer(step)},
            device_id_type=MESH,
        )

    def out_arrival(head, source):
        return pltpu.make_async_remote_copy(
            src_ref=result.at[head, rows_of(source)],
            dst_ref=out_ref.at[:, columns_of(source, head)],
            send_sem=out_send.at[head, 0],
            recv_sem=out_recv.at[head, source],
            device_id={"seq": source},
            device_id_type=MESH,
        )

    def out_own(head):
        return pltpu.make_async_copy(
            result.at[head, rows_of(me)],
            out_ref.at[:, columns_of(me, head)],
            out_send.at[head, 0],
        )

    barrier = pltpu.get_barrier_semaphore()
    for step in range(1, seq_count):
        pl.semaphore_signal(barrier, inc=1, device_id={"seq": peer(step)}, device_id_type=MESH)

    @pl.when(stage > 0)
    def _():
        for step in range(seq_count):
            pl.semaphore_signal(
                barrier, inc=1, device_id={"pipe": stage - 1, "seq": peer(step)}, device_id_type=MESH
            )

    @pl.when(stage < last)
    def _():
        for step in range(seq_count):
            pl.semaphore_signal(
                barrier, inc=1, device_id={"pipe": stage + 1, "seq": peer(step)}, device_id_type=MESH
            )

    @pl.when(stage == 0)
    def _():
        own_latent().start()

    neighbours = (
        seq_count - 1
        + jnp.where(stage > 0, seq_count, 0)
        + jnp.where(stage < last, seq_count, 0)
    )
    pl.semaphore_wait(barrier, neighbours)

    @pl.when(stage == 0)
    def _():
        for copy in latent_sends_x():
            copy.start()

    @pl.when(stage == helper)
    def _():
        for copy in latent_sends_y():
            copy.start()

    stale_copy().start()
    for part in range(3):
        weight_copy(part).start()

    picked_step = lax.broadcasted_iota(jnp.int32, modulation_ref.shape[1:], 0) == timestep_ref[0]
    for part in range(3):
        row = jnp.sum(jnp.where(picked_step, modulation_ref[part], 0.0), axis=0, keepdims=True)
        mods[pl.ds(part, 1), :] = row + 1.0 if part == 1 else row

    def normalize_rows(rows, block_rows):
        floated = block_rows.astype(jnp.float32)
        centred = floated - jnp.mean(floated, axis=-1, keepdims=True)
        spread = jnp.mean(centred * centred, axis=-1, keepdims=True)
        normed[rows, :] = (
            centred * lax.rsqrt(spread + EPSILON) * mods[1:2, :] + mods[0:1, :]
        ).astype(jnp.bfloat16)

    def row_chunks(source):
        for part in range(block // ROW_CHUNK):
            yield pl.ds(pl.multiple_of(source * block + part * ROW_CHUNK, ROW_CHUNK), ROW_CHUNK)

    def normalize_latent(source):
        for rows in row_chunks(source):
            block_rows = arrived[rows, :]
            normalize_rows(rows, block_rows)
            for place in range(columns):
                hidden[place, rows, :] = block_rows[:, place * HEAD_DIM : (place + 1) * HEAD_DIM]

    @pl.when(stage == 0)
    def _():
        own_latent().wait()
        normalize_latent(me)
        for source, half, copy in zip((across_x, across_y), (0, 1), latent_passes()):
            latent_pass(0, source, half, me).wait_recv()
            copy.start()

    key_tile = lax.broadcasted_iota(jnp.int32, (ntiles, ntiles), 0)
    query_tile = lax.broadcasted_iota(jnp.int32, (ntiles, ntiles), 1)
    chosen = jnp.zeros((ntiles, ntiles), jnp.float32)
    for j in range(tiles_ref.shape[0]):
        chosen = chosen + jnp.where(tiles_ref[pl.ds(j, 1), :] == key_tile, 1.0, 0.0)
    key_place = jnp.zeros((ntiles, ntiles), jnp.int32)
    query_place = jnp.zeros((ntiles, ntiles), jnp.int32)
    for t in range(patches):
        key_place = jnp.where(lax.div(key_tile, TILES_P) == order_ref[t], t, key_place)
        query_place = jnp.where(lax.div(query_tile, TILES_P) == order_ref[t], t, query_place)
    fresh = jnp.where(key_place <= query_place, chosen, 0.0)

    row_id = lax.broadcasted_iota(jnp.int32, (tokens, ntiles), 0)
    tile_id = lax.broadcasted_iota(jnp.int32, (tokens, ntiles), 1)
    in_block = lax.rem(row_id, block)
    token = lax.div(row_id, block) * rows_dev + lax.rem(in_block, rows_dev)
    tile_of_row = lax.div(in_block, rows_dev) * TILES_P + lax.div(token, tile_len)
    by_seq = jnp.where(tile_of_row == tile_id, 1.0, 0.0).astype(jnp.bfloat16)
    by_patch = jnp.where(lax.div(row_id, tile_len) == tile_id, 1.0, 0.0).astype(jnp.bfloat16)
    for place, (table, keys) in enumerate(((fresh, by_seq), (chosen - fresh, by_patch))):
        per_query = dot_t(by_seq, table.astype(jnp.bfloat16), ((1,), (1,)))
        seen = dot_t(per_query.astype(jnp.bfloat16), keys, ((1,), (1,)))
        bias[place] = (seen - 1.0) * MASKED

    stale_copy().wait()
    mixed_stale[...] = raw_stale[...].reshape(2 * tokens, local_w)
    wanted = 2 * lax.broadcasted_iota(jnp.int32, (tokens, 2 * tokens), 0)
    present = lax.broadcasted_iota(jnp.int32, (tokens, 2 * tokens), 1)
    for part in range(2):
        select = jnp.where(wanted + part == present, 1.0, 0.0).astype(jnp.bfloat16)
        stale[part] = jnp.dot(
            select, mixed_stale[...], preferred_element_type=jnp.float32
        ).astype(jnp.bfloat16)

    @pl.when(stage > 0)
    def _():
        def pass_on(head, carry):
            for source, half, copy in zip((across_x, across_y), (0, 1), next_passes(head)):
                next_pass(head, 0, source, half, across_x).wait_recv()
                copy.start()
            return carry

        def arrive(head, carry):
            for source, half in (
                (me, 0),
                (me, 1),
                (across_x, 1),
                (across_y, 0),
                (diagonal, 0),
                (diagonal, 1),
            ):
                next_pass(head, 0, source, half, across_x).wait_recv()
            return carry

        lax.fori_loop(0, heads, pass_on, 0)
        lax.fori_loop(0, heads, arrive, 0)
        each_back(lambda place: back_copy(place, stage - 1).start())

    @pl.when(stage == 0)
    def _():
        latent_pass(0, across_x, 1, across_y).wait_recv()
        normalize_latent(across_x)
        latent_pass(0, across_y, 0, across_x).wait_recv()
        normalize_latent(across_y)
        latent_pass(0, diagonal, 0, across_x).wait_recv()
        latent_pass(0, diagonal, 1, across_x).wait_recv()
        normalize_latent(diagonal)

    @pl.when(stage > 0)
    def _():
        def normalize_block(source, carry):
            for rows in row_chunks(source):
                normalize_rows(
                    rows,
                    jnp.concatenate([hidden[place, rows, :] for place in range(columns)], axis=1),
                )
            return carry

        lax.fori_loop(0, seq_count, normalize_block, 0)

    for part in range(3):
        weight_copy(part).wait()

    def project(group):
        lanes = slice(group[0] * HEAD_DIM, (group[-1] + 1) * HEAD_DIM)
        span = len(group) * HEAD_DIM
        pieces = [weights[part, :, lanes] for part in range(3)]
        if len(group) == 1:
            pieces = [jnp.concatenate(pieces, axis=1)]
        projected = [
            jnp.dot(normed[...], piece, preferred_element_type=jnp.float32) for piece in pieces
        ]
        for part in range(3):
            whole = (
                projected[part]
                if len(projected) == 3
                else projected[0][:, part * span : (part + 1) * span]
            )
            if part == 0:
                whole = whole * (HEAD_DIM ** (-0.5) * LOG2E)
            for place, head in enumerate(group):
                qkv[head, part] = whole[:, place * HEAD_DIM : (place + 1) * HEAD_DIM].astype(
                    jnp.bfloat16
                )

    def attend(head):
        query = qkv[head, 0]
        lanes = slice(head * HEAD_DIM, (head + 1) * HEAD_DIM)
        fresh_s = dot_t(query, qkv[head, 1], ((1,), (1,))) + bias[0]
        stale_s = dot_t(query, stale[0, :, lanes], ((1,), (1,))) + bias[1]
        largest = jnp.maximum(
            jnp.max(fresh_s, axis=-1, keepdims=True), jnp.max(stale_s, axis=-1, keepdims=True)
        )
        fresh_p = jnp.exp2(fresh_s - largest)
        stale_p = jnp.exp2(stale_s - largest)
        total = jnp.sum(fresh_p, axis=-1, keepdims=True) + jnp.sum(stale_p, axis=-1, keepdims=True)
        mixed = jnp.dot(
            fresh_p.astype(jnp.bfloat16), qkv[head, 2], preferred_element_type=jnp.float32
        ) + jnp.dot(
            stale_p.astype(jnp.bfloat16), stale[1, :, lanes], preferred_element_type=jnp.float32
        )
        attended = (mixed / total).astype(jnp.bfloat16).astype(jnp.float32)
        mine = columns_of(me, head)
        result[head] = (
            hidden[place_of(me, head)].astype(jnp.float32) + mods[2:3, mine] * attended
        ).astype(jnp.bfloat16)

    def send(head):
        @pl.when(stage < last)
        def _():
            for copy in next_sends(head):
                copy.start()

        @pl.when(stage == last)
        def _():
            for step in range(1, seq_count):
                out_copy(head, step).start()
            out_own(head).start()

    groups = [tuple(range(head, min(head + 2, heads))) for head in range(0, heads, 2)]
    project(groups[0])
    for place, group in enumerate(groups):
        if place + 1 < len(groups):
            project(groups[place + 1])
        for head in group:
            attend(head)
        for head in group:
            send(head)

    @pl.when(stage == 0)
    def _():
        for copy in latent_sends_x() + latent_passes():
            copy.wait_send()

    @pl.when(stage == helper)
    def _():
        for copy in latent_sends_y():
            copy.wait_send()

    @pl.when(stage > 0)
    def _():
        each_back(lambda place: back_copy(place, stage - 1).wait_send())

        def passed(head, carry):
            for copy in next_passes(head):
                copy.wait_send()
            return carry

        lax.fori_loop(0, heads, passed, 0)

    @pl.when(stage < last)
    def _():
        def sent(head, carry):
            for copy in next_sends(head):
                copy.wait_send()
            return carry

        lax.fori_loop(0, heads, sent, 0)
        each_back(lambda place: back_copy(place, stage + 1).wait_recv())

    @pl.when(stage == last)
    def _():
        def done(head, carry):
            out_own(head).wait()
            for step in range(1, seq_count):
                out_copy(head, step).wait_send()
                out_arrival(head, peer(step)).wait_recv()
            return carry

        lax.fori_loop(0, heads, done, 0)


def local(latent, w_qkv, modulation, timestep, order, tiles, stale_kv):
    patches, rows_dev, width = latent.shape
    local_w = w_qkv.shape[3]
    heads = local_w // HEAD_DIM
    seq_count = lax.axis_size("seq")
    pipe_count = lax.axis_size("pipe")
    block = patches * rows_dev
    tokens = block * seq_count
    weights = jnp.transpose(w_qkv[0], (1, 0, 2))
    stale = stale_kv[0].reshape(tokens, 2, local_w)
    mods = jnp.transpose(modulation[0], (1, 0, 2))
    smem = pl.BlockSpec(memory_space=pltpu.SMEM)
    vmem = pl.BlockSpec(memory_space=pltpu.VMEM)
    anywhere = pl.BlockSpec(memory_space=pl.ANY)
    bf16 = jnp.bfloat16
    dma = pltpu.SemaphoreType.DMA
    finished = pl.pallas_call(
        functools.partial(kernel, (patches, rows_dev, seq_count, pipe_count, heads)),
        out_shape=jax.ShapeDtypeStruct((block, width), bf16),
        in_specs=[smem, smem, anywhere, anywhere, vmem, vmem, anywhere],
        out_specs=anywhere,
        scratch_shapes=[
            pltpu.VMEM((tokens, width), bf16),
            pltpu.VMEM((seq_count * heads, tokens, HEAD_DIM), bf16),
            pltpu.VMEM((tokens, width), bf16),
            pltpu.VMEM((3, width, local_w), bf16),
            pltpu.VMEM((tokens, 2, local_w), bf16),
            pltpu.VMEM((2 * tokens, local_w), bf16),
            pltpu.VMEM((2, tokens, local_w), bf16),
            pltpu.VMEM((8, width), jnp.float32),
            pltpu.VMEM((2, tokens, tokens), jnp.float32),
            pltpu.VMEM((heads, tokens, HEAD_DIM), bf16),
            pltpu.VMEM((heads, 3, tokens, HEAD_DIM), bf16),
            dma((3,)),
            dma(()),
            dma(()),
            dma((6,)),
            dma((seq_count, 2)),
            dma((heads, 6)),
            dma((heads, seq_count, 2)),
            dma((heads, 2)),
            dma((heads, seq_count)),
            dma((heads, seq_count)),
            dma((seq_count * heads,)),
            dma((seq_count * heads,)),
        ],
        compiler_params=pltpu.CompilerParams(
            collective_id=0, has_side_effects=True, vmem_limit_bytes=56 * 1024 * 1024
        ),
    )(timestep, order, latent.reshape(block, width), weights, mods, tiles.T, stale)
    return finished.reshape(1, patches, rows_dev, width)


def solution(mesh):
    return jax.shard_map(
        local,
        mesh=mesh,
        in_specs=(
            P("batch", "seq", None),
            P("pipe", None, None, "seq"),
            P("pipe", None, None, None),
            P(),
            P("batch"),
            P("batch", None),
            P("pipe", "batch", None, None, "seq"),
        ),
        out_specs=P("pipe", "batch", "seq", None),
        check_vma=False,
    )
```

```python
import functools

import jax
import jax.numpy as jnp
from jax import lax
from jax.experimental import pallas as pl
from jax.experimental.pallas import tpu as pltpu
from jax.sharding import PartitionSpec as P

HEAD_DIM = 128
TILES_P = 2
EPSILON = 1e-06
MASKED = 1e30
LOG2E = 1.4426950408889634
MESH = pl.DeviceIdType.MESH
ROW_CHUNK = 16


def dot_t(a, b, dims):
    return lax.dot_general(a, b, (dims, ((), ())), preferred_element_type=jnp.float32)


def kernel(
    sizes,
    timestep_ref,
    order_ref,
    latent_ref,
    weights_ref,
    modulation_ref,
    tiles_ref,
    stale_ref,
    out_ref,
    arrived,
    hidden,
    normed,
    weights,
    raw_stale,
    mixed_stale,
    stale,
    mods,
    bias,
    result,
    qkv,
    weight_sem,
    stale_sem,
    own_sem,
    lat_send,
    lat_recv,
    next_send,
    next_recv,
    pass_send,
    out_send,
    out_recv,
    back_send,
    back_recv,
    modulation,
    mods_sem,
):
    patches, rows_dev, seq_count, pipe_count, heads = sizes
    stage = lax.axis_index("pipe")
    me = lax.axis_index("seq")
    last = pipe_count - 1
    helper = min(1, last)
    block = patches * rows_dev
    tokens = block * seq_count
    local_w = heads * HEAD_DIM
    tile_len = rows_dev * seq_count // TILES_P
    ntiles = patches * TILES_P
    columns = seq_count * heads

    def rows_of(rank):
        return pl.ds(pl.multiple_of(rank * block, block), block)

    def columns_of(rank, head):
        return pl.ds(pl.multiple_of(rank * local_w + head * HEAD_DIM, HEAD_DIM), HEAD_DIM)

    def place_of(rank, head):
        return rank * heads + head

    square = 2
    across_x = lax.div(me, square) * square + (square - 1 - lax.rem(me, square))
    across_y = (square - 1 - lax.div(me, square)) * square + lax.rem(me, square)
    diagonal = seq_count - 1 - me

    def peer(step):
        return lax.rem(me + step, seq_count)

    def weight_copy(part):
        return pltpu.make_async_copy(weights_ref.at[part], weights.at[part], weight_sem.at[part])

    def stale_copy():
        return pltpu.make_async_copy(stale_ref, raw_stale, stale_sem)

    def own_latent():
        return pltpu.make_async_copy(latent_ref, arrived.at[rows_of(me)], own_sem)

    def half_of(rank, half, size):
        return pl.ds(pl.multiple_of(rank * size + half * (size // 2), size // 2), size // 2)

    def latent_copy(slot, half, target):
        return pltpu.make_async_remote_copy(
            src_ref=latent_ref.at[half_of(0, half, block)],
            dst_ref=arrived.at[half_of(me, half, block)],
            send_sem=lat_send.at[slot],
            recv_sem=lat_recv.at[me, half],
            device_id={"pipe": 0, "seq": target},
            device_id_type=MESH,
        )

    def latent_pass(slot, source, half, target):
        rows = half_of(source, half, block)
        return pltpu.make_async_remote_copy(
            src_ref=arrived.at[rows],
            dst_ref=arrived.at[rows],
            send_sem=lat_send.at[slot],
            recv_sem=lat_recv.at[source, half],
            device_id={"seq": target},
            device_id_type=MESH,
        )

    def latent_sends_x():
        return latent_copy(0, 0, across_x), latent_copy(2, 1, across_x)

    def latent_sends_y():
        return latent_copy(1, 1, across_y), latent_copy(3, 0, across_y)

    def latent_passes():
        return latent_pass(4, across_x, 0, across_y), latent_pass(5, across_y, 1, across_x)

    def next_copy(head, slot, half, target):
        rows = half_of(0, half, tokens)
        return pltpu.make_async_remote_copy(
            src_ref=result.at[head, rows],
            dst_ref=hidden.at[place_of(me, head), rows],
            send_sem=next_send.at[head, slot],
            recv_sem=next_recv.at[head, me, half],
            device_id={"pipe": stage + 1, "seq": target},
            device_id_type=MESH,
        )

    def next_sends(head):
        return (
            next_copy(head, 0, 0, across_x),
            next_copy(head, 1, 1, across_y),
            next_copy(head, 2, 1, across_x),
            next_copy(head, 3, 0, across_y),
            next_copy(head, 4, 0, me),
            next_copy(head, 5, 1, me),
        )

    def next_pass(head, slot, source, half, target):
        place = hidden.at[place_of(source, head), half_of(0, half, tokens)]
        return pltpu.make_async_remote_copy(
            src_ref=place,
            dst_ref=place,
            send_sem=pass_send.at[head, slot],
            recv_sem=next_recv.at[head, source, half],
            device_id={"seq": target},
            device_id_type=MESH,
        )

    def next_passes(head):
        return (
            next_pass(head, 0, across_x, 0, across_y),
            next_pass(head, 1, across_y, 1, across_x),
        )

    def back_copy(target):
        return pltpu.make_async_remote_copy(
            src_ref=arrived.at[rows_of(me)],
            dst_ref=out_ref,
            send_sem=back_send,
            recv_sem=back_recv,
            device_id={"pipe": target},
            device_id_type=MESH,
        )

    def mods_copy():
        return pltpu.make_async_copy(modulation_ref, modulation, mods_sem)

    def out_copy(head, step):
        return pltpu.make_async_remote_copy(
            src_ref=result.at[head, rows_of(peer(step))],
            dst_ref=out_ref.at[:, columns_of(me, head)],
            send_sem=out_send.at[head, step],
            recv_sem=out_recv.at[head, me],
            device_id={"seq": peer(step)},
            device_id_type=MESH,
        )

    def out_arrival(head, source):
        return pltpu.make_async_remote_copy(
            src_ref=result.at[head, rows_of(source)],
            dst_ref=out_ref.at[:, columns_of(source, head)],
            send_sem=out_send.at[head, 0],
            recv_sem=out_recv.at[head, source],
            device_id={"seq": source},
            device_id_type=MESH,
        )

    def out_own(head):
        return pltpu.make_async_copy(
            result.at[head, rows_of(me)],
            out_ref.at[:, columns_of(me, head)],
            out_send.at[head, 0],
        )

    barrier = pltpu.get_barrier_semaphore()
    for step in range(1, seq_count):
        pl.semaphore_signal(barrier, inc=1, device_id={"seq": peer(step)}, device_id_type=MESH)

    @pl.when(stage > 0)
    def _():
        for step in range(seq_count):
            pl.semaphore_signal(
                barrier, inc=1, device_id={"pipe": stage - 1, "seq": peer(step)}, device_id_type=MESH
            )

    @pl.when(stage < last)
    def _():
        for step in range(seq_count):
            pl.semaphore_signal(
                barrier, inc=1, device_id={"pipe": stage + 1, "seq": peer(step)}, device_id_type=MESH
            )

    mods_copy().start()

    @pl.when(stage == 0)
    def _():
        own_latent().start()

    neighbours = (
        seq_count - 1
        + jnp.where(stage > 0, seq_count, 0)
        + jnp.where(stage < last, seq_count, 0)
    )
    pl.semaphore_wait(barrier, neighbours)

    @pl.when(stage == 0)
    def _():
        for copy in latent_sends_x():
            copy.start()

    @pl.when(stage == helper)
    def _():
        for copy in latent_sends_y():
            copy.start()

    stale_copy().start()
    for part in range(3):
        weight_copy(part).start()

    mods_copy().wait()
    picked_step = lax.broadcasted_iota(jnp.int32, modulation.shape[1:], 0) == timestep_ref[0]
    for part in range(3):
        row = jnp.sum(jnp.where(picked_step, modulation[part], 0.0), axis=0, keepdims=True)
        mods[pl.ds(part, 1), :] = row + 1.0 if part == 1 else row

    def normalize_rows(rows, block_rows):
        floated = block_rows.astype(jnp.float32)
        centred = floated - jnp.mean(floated, axis=-1, keepdims=True)
        spread = jnp.mean(centred * centred, axis=-1, keepdims=True)
        normed[rows, :] = (
            centred * lax.rsqrt(spread + EPSILON) * mods[1:2, :] + mods[0:1, :]
        ).astype(jnp.bfloat16)

    def row_chunks(source):
        for part in range(block // ROW_CHUNK):
            yield pl.ds(pl.multiple_of(source * block + part * ROW_CHUNK, ROW_CHUNK), ROW_CHUNK)

    def normalize_latent(source):
        for rows in row_chunks(source):
            block_rows = arrived[rows, :]
            normalize_rows(rows, block_rows)
            for place in range(columns):
                hidden[place, rows, :] = block_rows[:, place * HEAD_DIM : (place + 1) * HEAD_DIM]

    @pl.when(stage == 0)
    def _():
        own_latent().wait()
        normalize_latent(me)
        for source, half, copy in zip((across_x, across_y), (0, 1), latent_passes()):
            latent_pass(0, source, half, me).wait_recv()
            copy.start()

    key_tile = lax.broadcasted_iota(jnp.int32, (ntiles, ntiles), 0)
    query_tile = lax.broadcasted_iota(jnp.int32, (ntiles, ntiles), 1)
    chosen = jnp.zeros((ntiles, ntiles), jnp.float32)
    for j in range(tiles_ref.shape[0]):
        chosen = chosen + jnp.where(tiles_ref[pl.ds(j, 1), :] == key_tile, 1.0, 0.0)
    key_place = jnp.zeros((ntiles, ntiles), jnp.int32)
    query_place = jnp.zeros((ntiles, ntiles), jnp.int32)
    for t in range(patches):
        key_place = jnp.where(lax.div(key_tile, TILES_P) == order_ref[t], t, key_place)
        query_place = jnp.where(lax.div(query_tile, TILES_P) == order_ref[t], t, query_place)
    fresh = jnp.where(key_place <= query_place, chosen, 0.0)

    row_id = lax.broadcasted_iota(jnp.int32, (tokens, ntiles), 0)
    tile_id = lax.broadcasted_iota(jnp.int32, (tokens, ntiles), 1)
    in_block = lax.rem(row_id, block)
    token = lax.div(row_id, block) * rows_dev + lax.rem(in_block, rows_dev)
    tile_of_row = lax.div(in_block, rows_dev) * TILES_P + lax.div(token, tile_len)
    by_seq = jnp.where(tile_of_row == tile_id, 1.0, 0.0).astype(jnp.bfloat16)
    by_patch = jnp.where(lax.div(row_id, tile_len) == tile_id, 1.0, 0.0).astype(jnp.bfloat16)
    for place, (table, keys) in enumerate(((fresh, by_seq), (chosen - fresh, by_patch))):
        per_query = dot_t(by_seq, table.astype(jnp.bfloat16), ((1,), (1,)))
        seen = dot_t(per_query.astype(jnp.bfloat16), keys, ((1,), (1,)))
        bias[place] = (seen - 1.0) * MASKED

    stale_copy().wait()
    mixed_stale[...] = raw_stale[...].reshape(2 * tokens, local_w)
    wanted = 2 * lax.broadcasted_iota(jnp.int32, (tokens, 2 * tokens), 0)
    present = lax.broadcasted_iota(jnp.int32, (tokens, 2 * tokens), 1)
    for part in range(2):
        select = jnp.where(wanted + part == present, 1.0, 0.0).astype(jnp.bfloat16)
        stale[part] = jnp.dot(
            select, mixed_stale[...], preferred_element_type=jnp.float32
        ).astype(jnp.bfloat16)

    @pl.when(stage > 0)
    def _():
        def pass_on(head, carry):
            for source, half, copy in zip((across_x, across_y), (0, 1), next_passes(head)):
                next_pass(head, 0, source, half, across_x).wait_recv()
                copy.start()
            return carry

        def arrive(head, carry):
            for source, half in (
                (me, 0),
                (me, 1),
                (across_x, 1),
                (across_y, 0),
                (diagonal, 0),
                (diagonal, 1),
            ):
                next_pass(head, 0, source, half, across_x).wait_recv()
            return carry

        lax.fori_loop(0, heads, pass_on, 0)
        lax.fori_loop(0, heads, arrive, 0)

    @pl.when(stage == 0)
    def _():
        latent_pass(0, across_x, 1, across_y).wait_recv()
        normalize_latent(across_x)
        latent_pass(0, across_y, 0, across_x).wait_recv()
        normalize_latent(across_y)
        latent_pass(0, diagonal, 0, across_x).wait_recv()
        latent_pass(0, diagonal, 1, across_x).wait_recv()
        normalize_latent(diagonal)

    @pl.when(stage > 0)
    def _():
        def normalize_block(source, carry):
            for rows in row_chunks(source):
                normalize_rows(
                    rows,
                    jnp.concatenate([hidden[place, rows, :] for place in range(columns)], axis=1),
                )
            return carry

        lax.fori_loop(0, seq_count, normalize_block, 0)
        for rows in row_chunks(me):
            arrived[rows, :] = jnp.concatenate(
                [hidden[place, rows, :] for place in range(columns)], axis=1
            )
        back_copy(stage - 1).start()

    for part in range(3):
        weight_copy(part).wait()

    def project(group):
        lanes = slice(group[0] * HEAD_DIM, (group[-1] + 1) * HEAD_DIM)
        span = len(group) * HEAD_DIM
        pieces = [weights[part, :, lanes] for part in range(3)]
        if len(group) == 1:
            pieces = [jnp.concatenate(pieces, axis=1)]
        projected = [
            jnp.dot(normed[...], piece, preferred_element_type=jnp.float32) for piece in pieces
        ]
        for part in range(3):
            whole = (
                projected[part]
                if len(projected) == 3
                else projected[0][:, part * span : (part + 1) * span]
            )
            if part == 0:
                whole = whole * (HEAD_DIM ** (-0.5) * LOG2E)
            for place, head in enumerate(group):
                qkv[head, part] = whole[:, place * HEAD_DIM : (place + 1) * HEAD_DIM].astype(
                    jnp.bfloat16
                )

    def attend(head):
        query = qkv[head, 0]
        lanes = slice(head * HEAD_DIM, (head + 1) * HEAD_DIM)
        fresh_s = dot_t(query, qkv[head, 1], ((1,), (1,))) + bias[0]
        stale_s = dot_t(query, stale[0, :, lanes], ((1,), (1,))) + bias[1]
        largest = jnp.maximum(
            jnp.max(fresh_s, axis=-1, keepdims=True), jnp.max(stale_s, axis=-1, keepdims=True)
        )
        fresh_p = jnp.exp2(fresh_s - largest)
        stale_p = jnp.exp2(stale_s - largest)
        total = jnp.sum(fresh_p, axis=-1, keepdims=True) + jnp.sum(stale_p, axis=-1, keepdims=True)
        mixed = jnp.dot(
            fresh_p.astype(jnp.bfloat16), qkv[head, 2], preferred_element_type=jnp.float32
        ) + jnp.dot(
            stale_p.astype(jnp.bfloat16), stale[1, :, lanes], preferred_element_type=jnp.float32
        )
        attended = (mixed / total).astype(jnp.bfloat16).astype(jnp.float32)
        mine = columns_of(me, head)
        result[head] = (
            hidden[place_of(me, head)].astype(jnp.float32) + mods[2:3, mine] * attended
        ).astype(jnp.bfloat16)

    def send(head):
        @pl.when(stage < last)
        def _():
            for copy in next_sends(head):
                copy.start()

        @pl.when(stage == last)
        def _():
            for step in range(1, seq_count):
                out_copy(head, step).start()
            out_own(head).start()

    groups = [tuple(range(head, min(head + 2, heads))) for head in range(0, heads, 2)]
    project(groups[0])
    for place, group in enumerate(groups):
        if place + 1 < len(groups):
            project(groups[place + 1])
        for head in group:
            attend(head)
        for head in group:
            send(head)

    @pl.when(stage == 0)
    def _():
        for copy in latent_sends_x() + latent_passes():
            copy.wait_send()

    @pl.when(stage == helper)
    def _():
        for copy in latent_sends_y():
            copy.wait_send()

    @pl.when(stage > 0)
    def _():
        back_copy(stage - 1).wait_send()

        def passed(head, carry):
            for copy in next_passes(head):
                copy.wait_send()
            return carry

        lax.fori_loop(0, heads, passed, 0)

    @pl.when(stage < last)
    def _():
        def sent(head, carry):
            for copy in next_sends(head):
                copy.wait_send()
            return carry

        lax.fori_loop(0, heads, sent, 0)
        back_copy(stage + 1).wait_recv()

    @pl.when(stage == last)
    def _():
        def done(head, carry):
            out_own(head).wait()
            for step in range(1, seq_count):
                out_copy(head, step).wait_send()
                out_arrival(head, peer(step)).wait_recv()
            return carry

        lax.fori_loop(0, heads, done, 0)


def local(latent, w_qkv, modulation, timestep, order, tiles, stale_kv):
    patches, rows_dev, width = latent.shape
    local_w = w_qkv.shape[3]
    heads = local_w // HEAD_DIM
    seq_count = lax.axis_size("seq")
    pipe_count = lax.axis_size("pipe")
    block = patches * rows_dev
    tokens = block * seq_count
    weights = jnp.transpose(w_qkv[0], (1, 0, 2))
    stale = stale_kv[0].reshape(tokens, 2, local_w)
    mods = jnp.transpose(modulation[0], (1, 0, 2))
    smem = pl.BlockSpec(memory_space=pltpu.SMEM)
    vmem = pl.BlockSpec(memory_space=pltpu.VMEM)
    anywhere = pl.BlockSpec(memory_space=pl.ANY)
    bf16 = jnp.bfloat16
    dma = pltpu.SemaphoreType.DMA
    finished = pl.pallas_call(
        functools.partial(kernel, (patches, rows_dev, seq_count, pipe_count, heads)),
        out_shape=jax.ShapeDtypeStruct((block, width), bf16),
        in_specs=[smem, smem, anywhere, anywhere, anywhere, vmem, anywhere],
        out_specs=anywhere,
        scratch_shapes=[
            pltpu.VMEM((tokens, width), bf16),
            pltpu.VMEM((seq_count * heads, tokens, HEAD_DIM), bf16),
            pltpu.VMEM((tokens, width), bf16),
            pltpu.VMEM((3, width, local_w), bf16),
            pltpu.VMEM((tokens, 2, local_w), bf16),
            pltpu.VMEM((2 * tokens, local_w), bf16),
            pltpu.VMEM((2, tokens, local_w), bf16),
            pltpu.VMEM((8, width), jnp.float32),
            pltpu.VMEM((2, tokens, tokens), jnp.float32),
            pltpu.VMEM((heads, tokens, HEAD_DIM), bf16),
            pltpu.VMEM((heads, 3, tokens, HEAD_DIM), bf16),
            dma((3,)),
            dma(()),
            dma(()),
            dma((6,)),
            dma((seq_count, 2)),
            dma((heads, 6)),
            dma((heads, seq_count, 2)),
            dma((heads, 2)),
            dma((heads, seq_count)),
            dma((heads, seq_count)),
            dma(()),
            dma(()),
            pltpu.VMEM(mods.shape, jnp.float32),
            dma(()),
        ],
        compiler_params=pltpu.CompilerParams(
            collective_id=0, has_side_effects=True, vmem_limit_bytes=56 * 1024 * 1024
        ),
    )(timestep, order, latent.reshape(block, width), weights, mods, tiles.T, stale)
    return finished.reshape(1, patches, rows_dev, width)


def solution(mesh):
    return jax.shard_map(
        local,
        mesh=mesh,
        in_specs=(
            P("batch", "seq", None),
            P("pipe", None, None, "seq"),
            P("pipe", None, None, None),
            P(),
            P("batch"),
            P("batch", None),
            P("pipe", "batch", None, None, "seq"),
        ),
        out_specs=P("pipe", "batch", "seq", None),
        check_vma=False,
    )
```

```python
import functools

import jax
import jax.numpy as jnp
from jax import lax
from jax.experimental import pallas as pl
from jax.experimental.pallas import tpu as pltpu
from jax.sharding import PartitionSpec as P

HEAD_DIM = 128
TILES_P = 2
EPSILON = 1e-06
MASKED = 1e30
LOG2E = 1.4426950408889634
MESH = pl.DeviceIdType.MESH
ROW_CHUNK = 16


def dot_t(a, b, dims):
    return lax.dot_general(a, b, (dims, ((), ())), preferred_element_type=jnp.float32)


def kernel(
    sizes,
    timestep_ref,
    order_ref,
    latent_ref,
    weights_ref,
    modulation_ref,
    tiles_ref,
    stale_ref,
    out_ref,
    arrived,
    hidden,
    normed,
    weights,
    raw_stale,
    mixed_stale,
    stale,
    mods,
    bias,
    result,
    qkv,
    weight_sem,
    stale_sem,
    own_sem,
    lat_send,
    lat_recv,
    next_send,
    next_recv,
    pass_send,
    out_send,
    out_recv,
    back_send,
    back_recv,
    modulation,
    mods_sem,
):
    patches, rows_dev, seq_count, pipe_count, heads = sizes
    stage = lax.axis_index("pipe")
    me = lax.axis_index("seq")
    last = pipe_count - 1
    helper = min(1, last)
    block = patches * rows_dev
    tokens = block * seq_count
    local_w = heads * HEAD_DIM
    tile_len = rows_dev * seq_count // TILES_P
    ntiles = patches * TILES_P
    columns = seq_count * heads

    def rows_of(rank):
        return pl.ds(pl.multiple_of(rank * block, block), block)

    def columns_of(rank, head):
        return pl.ds(pl.multiple_of(rank * local_w + head * HEAD_DIM, HEAD_DIM), HEAD_DIM)

    def place_of(rank, head):
        return rank * heads + head

    square = 2
    across_x = lax.div(me, square) * square + (square - 1 - lax.rem(me, square))
    across_y = (square - 1 - lax.div(me, square)) * square + lax.rem(me, square)
    diagonal = seq_count - 1 - me

    def peer(step):
        return lax.rem(me + step, seq_count)

    def weight_copy(part):
        return pltpu.make_async_copy(weights_ref.at[part], weights.at[part], weight_sem.at[part])

    def stale_copy():
        return pltpu.make_async_copy(stale_ref, raw_stale, stale_sem)

    def own_latent():
        return pltpu.make_async_copy(latent_ref, arrived.at[rows_of(me)], own_sem)

    def half_of(rank, half, size):
        return pl.ds(pl.multiple_of(rank * size + half * (size // 2), size // 2), size // 2)

    def latent_copy(slot, half, target):
        return pltpu.make_async_remote_copy(
            src_ref=latent_ref.at[half_of(0, half, block)],
            dst_ref=arrived.at[half_of(me, half, block)],
            send_sem=lat_send.at[slot],
            recv_sem=lat_recv.at[me, half],
            device_id={"pipe": 0, "seq": target},
            device_id_type=MESH,
        )

    def latent_pass(slot, source, half, target):
        rows = half_of(source, half, block)
        return pltpu.make_async_remote_copy(
            src_ref=arrived.at[rows],
            dst_ref=arrived.at[rows],
            send_sem=lat_send.at[slot],
            recv_sem=lat_recv.at[source, half],
            device_id={"seq": target},
            device_id_type=MESH,
        )

    def latent_sends_x():
        return latent_copy(0, 0, across_x), latent_copy(2, 1, across_x)

    def latent_sends_y():
        return latent_copy(1, 1, across_y), latent_copy(3, 0, across_y)

    def latent_passes():
        return latent_pass(4, across_x, 0, across_y), latent_pass(5, across_y, 1, across_x)

    def next_copy(head, slot, half, target):
        rows = half_of(0, half, tokens)
        return pltpu.make_async_remote_copy(
            src_ref=result.at[head, rows],
            dst_ref=hidden.at[place_of(me, head), rows],
            send_sem=next_send.at[head, slot],
            recv_sem=next_recv.at[head, me, half],
            device_id={"pipe": stage + 1, "seq": target},
            device_id_type=MESH,
        )

    def next_sends(head):
        return (
            next_copy(head, 0, 0, across_x),
            next_copy(head, 1, 1, across_y),
            next_copy(head, 2, 1, across_x),
            next_copy(head, 3, 0, across_y),
            next_copy(head, 4, 0, me),
            next_copy(head, 5, 1, me),
        )

    def next_pass(head, slot, source, half, target):
        place = hidden.at[place_of(source, head), half_of(0, half, tokens)]
        return pltpu.make_async_remote_copy(
            src_ref=place,
            dst_ref=place,
            send_sem=pass_send.at[head, slot],
            recv_sem=next_recv.at[head, source, half],
            device_id={"seq": target},
            device_id_type=MESH,
        )

    def next_passes(head):
        return (
            next_pass(head, 0, across_x, 0, across_y),
            next_pass(head, 1, across_y, 1, across_x),
        )

    def back_copy(target):
        return pltpu.make_async_remote_copy(
            src_ref=arrived.at[rows_of(me)],
            dst_ref=out_ref,
            send_sem=back_send,
            recv_sem=back_recv,
            device_id={"pipe": target},
            device_id_type=MESH,
        )

    def mods_copy():
        return pltpu.make_async_copy(modulation_ref, modulation, mods_sem)

    def out_copy(head, step):
        return pltpu.make_async_remote_copy(
            src_ref=result.at[head, rows_of(peer(step))],
            dst_ref=out_ref.at[:, columns_of(me, head)],
            send_sem=out_send.at[head, step],
            recv_sem=out_recv.at[head, me],
            device_id={"seq": peer(step)},
            device_id_type=MESH,
        )

    def out_arrival(head, source):
        return pltpu.make_async_remote_copy(
            src_ref=result.at[head, rows_of(source)],
            dst_ref=out_ref.at[:, columns_of(source, head)],
            send_sem=out_send.at[head, 0],
            recv_sem=out_recv.at[head, source],
            device_id={"seq": source},
            device_id_type=MESH,
        )

    def out_own(head):
        return pltpu.make_async_copy(
            result.at[head, rows_of(me)],
            out_ref.at[:, columns_of(me, head)],
            out_send.at[head, 0],
        )

    barrier = pltpu.get_barrier_semaphore()
    for step in range(1, seq_count):
        pl.semaphore_signal(barrier, inc=1, device_id={"seq": peer(step)}, device_id_type=MESH)

    @pl.when(stage > 0)
    def _():
        for step in range(seq_count):
            pl.semaphore_signal(
                barrier, inc=1, device_id={"pipe": stage - 1, "seq": peer(step)}, device_id_type=MESH
            )

    @pl.when(stage < last)
    def _():
        for step in range(seq_count):
            pl.semaphore_signal(
                barrier, inc=1, device_id={"pipe": stage + 1, "seq": peer(step)}, device_id_type=MESH
            )

    mods_copy().start()

    @pl.when(stage == 0)
    def _():
        own_latent().start()

    neighbours = (
        seq_count - 1
        + jnp.where(stage > 0, seq_count, 0)
        + jnp.where(stage < last, seq_count, 0)
    )
    pl.semaphore_wait(barrier, neighbours)

    @pl.when(stage == 0)
    def _():
        for copy in latent_sends_x():
            copy.start()

    @pl.when(stage == helper)
    def _():
        for copy in latent_sends_y():
            copy.start()

    stale_copy().start()
    for part in range(3):
        weight_copy(part).start()

    mods_copy().wait()
    picked_step = lax.broadcasted_iota(jnp.int32, modulation.shape[1:], 0) == timestep_ref[0]
    for part in range(3):
        row = jnp.sum(jnp.where(picked_step, modulation[part], 0.0), axis=0, keepdims=True)
        mods[pl.ds(part, 1), :] = row + 1.0 if part == 1 else row

    def normalize_rows(rows, block_rows):
        floated = block_rows.astype(jnp.float32)
        centred = floated - jnp.mean(floated, axis=-1, keepdims=True)
        spread = jnp.mean(centred * centred, axis=-1, keepdims=True)
        normed[rows, :] = (
            centred * lax.rsqrt(spread + EPSILON) * mods[1:2, :] + mods[0:1, :]
        ).astype(jnp.bfloat16)

    def row_chunks(source):
        for part in range(block // ROW_CHUNK):
            yield pl.ds(pl.multiple_of(source * block + part * ROW_CHUNK, ROW_CHUNK), ROW_CHUNK)

    def normalize_latent(source):
        for rows in row_chunks(source):
            block_rows = arrived[rows, :]
            normalize_rows(rows, block_rows)
            for place in range(columns):
                hidden[place, rows, :] = block_rows[:, place * HEAD_DIM : (place + 1) * HEAD_DIM]

    @pl.when(stage == 0)
    def _():
        own_latent().wait()
        normalize_latent(me)
        for source, half, copy in zip((across_x, across_y), (0, 1), latent_passes()):
            latent_pass(0, source, half, me).wait_recv()
            copy.start()

    key_tile = lax.broadcasted_iota(jnp.int32, (ntiles, ntiles), 0)
    query_tile = lax.broadcasted_iota(jnp.int32, (ntiles, ntiles), 1)
    chosen = jnp.zeros((ntiles, ntiles), jnp.float32)
    for j in range(tiles_ref.shape[0]):
        chosen = chosen + jnp.where(tiles_ref[pl.ds(j, 1), :] == key_tile, 1.0, 0.0)
    key_place = jnp.zeros((ntiles, ntiles), jnp.int32)
    query_place = jnp.zeros((ntiles, ntiles), jnp.int32)
    for t in range(patches):
        key_place = jnp.where(lax.div(key_tile, TILES_P) == order_ref[t], t, key_place)
        query_place = jnp.where(lax.div(query_tile, TILES_P) == order_ref[t], t, query_place)
    fresh = jnp.where(key_place <= query_place, chosen, 0.0)

    row_id = lax.broadcasted_iota(jnp.int32, (tokens, ntiles), 0)
    tile_id = lax.broadcasted_iota(jnp.int32, (tokens, ntiles), 1)
    in_block = lax.rem(row_id, block)
    token = lax.div(row_id, block) * rows_dev + lax.rem(in_block, rows_dev)
    tile_of_row = lax.div(in_block, rows_dev) * TILES_P + lax.div(token, tile_len)
    by_seq = jnp.where(tile_of_row == tile_id, 1.0, 0.0).astype(jnp.bfloat16)
    by_patch = jnp.where(lax.div(row_id, tile_len) == tile_id, 1.0, 0.0).astype(jnp.bfloat16)
    for place, (table, keys) in enumerate(((fresh, by_seq), (chosen - fresh, by_patch))):
        per_query = dot_t(by_seq, table.astype(jnp.bfloat16), ((1,), (1,)))
        seen = dot_t(per_query.astype(jnp.bfloat16), keys, ((1,), (1,)))
        bias[place] = (seen - 1.0) * MASKED

    stale_copy().wait()
    mixed_stale[...] = raw_stale[...].reshape(2 * tokens, local_w)
    wanted = 2 * lax.broadcasted_iota(jnp.int32, (tokens, 2 * tokens), 0)
    present = lax.broadcasted_iota(jnp.int32, (tokens, 2 * tokens), 1)
    for part in range(2):
        select = jnp.where(wanted + part == present, 1.0, 0.0).astype(jnp.bfloat16)
        stale[part] = jnp.dot(
            select, mixed_stale[...], preferred_element_type=jnp.float32
        ).astype(jnp.bfloat16)

    @pl.when(stage > 0)
    def _():
        def pass_on(head, carry):
            for source, half, copy in zip((across_x, across_y), (0, 1), next_passes(head)):
                next_pass(head, 0, source, half, across_x).wait_recv()
                copy.start()
            return carry

        def arrive(head, carry):
            for source, half in (
                (me, 0),
                (me, 1),
                (across_x, 1),
                (across_y, 0),
                (diagonal, 0),
                (diagonal, 1),
            ):
                next_pass(head, 0, source, half, across_x).wait_recv()
            return carry

        lax.fori_loop(0, heads, pass_on, 0)
        lax.fori_loop(0, heads, arrive, 0)

    @pl.when(stage == 0)
    def _():
        latent_pass(0, across_x, 1, across_y).wait_recv()
        normalize_latent(across_x)
        latent_pass(0, across_y, 0, across_x).wait_recv()
        normalize_latent(across_y)
        latent_pass(0, diagonal, 0, across_x).wait_recv()
        latent_pass(0, diagonal, 1, across_x).wait_recv()
        normalize_latent(diagonal)

    @pl.when(stage > 0)
    def _():
        def normalize_block(source, carry):
            for rows in row_chunks(source):
                normalize_rows(
                    rows,
                    jnp.concatenate([hidden[place, rows, :] for place in range(columns)], axis=1),
                )
            return carry

        lax.fori_loop(0, seq_count, normalize_block, 0)
        for rows in row_chunks(me):
            arrived[rows, :] = jnp.concatenate(
                [hidden[place, rows, :] for place in range(columns)], axis=1
            )
        back_copy(stage - 1).start()

    for part in range(3):
        weight_copy(part).wait()

    def project(group):
        lanes = slice(group[0] * HEAD_DIM, (group[-1] + 1) * HEAD_DIM)
        span = len(group) * HEAD_DIM
        pieces = [weights[part, :, lanes] for part in range(3)]
        if len(group) == 1:
            pieces = [jnp.concatenate(pieces, axis=1)]
        projected = [
            jnp.dot(normed[...], piece, preferred_element_type=jnp.float32) for piece in pieces
        ]
        for part in range(3):
            whole = (
                projected[part]
                if len(projected) == 3
                else projected[0][:, part * span : (part + 1) * span]
            )
            if part == 0:
                whole = whole * (HEAD_DIM ** (-0.5) * LOG2E)
            for place, head in enumerate(group):
                qkv[head, part] = whole[:, place * HEAD_DIM : (place + 1) * HEAD_DIM].astype(
                    jnp.bfloat16
                )

    def attend(head):
        query = qkv[head, 0]
        lanes = slice(head * HEAD_DIM, (head + 1) * HEAD_DIM)
        fresh_s = dot_t(query, qkv[head, 1], ((1,), (1,))) + bias[0]
        stale_s = dot_t(query, stale[0, :, lanes], ((1,), (1,))) + bias[1]
        largest = jnp.maximum(
            jnp.max(fresh_s, axis=-1, keepdims=True), jnp.max(stale_s, axis=-1, keepdims=True)
        )
        fresh_p = jnp.exp2(fresh_s - largest)
        stale_p = jnp.exp2(stale_s - largest)
        total = jnp.sum(fresh_p, axis=-1, keepdims=True) + jnp.sum(stale_p, axis=-1, keepdims=True)
        mixed = jnp.dot(
            fresh_p.astype(jnp.bfloat16), qkv[head, 2], preferred_element_type=jnp.float32
        ) + jnp.dot(
            stale_p.astype(jnp.bfloat16), stale[1, :, lanes], preferred_element_type=jnp.float32
        )
        attended = (mixed / total).astype(jnp.bfloat16).astype(jnp.float32)
        mine = columns_of(me, head)
        result[head] = (
            hidden[place_of(me, head)].astype(jnp.float32) + mods[2:3, mine] * attended
        ).astype(jnp.bfloat16)

    def send(head):
        @pl.when(stage < last)
        def _():
            for copy in next_sends(head):
                copy.start()

        @pl.when(stage == last)
        def _():
            for step in range(1, seq_count):
                out_copy(head, step).start()
            out_own(head).start()

    groups = [(0,)] + [
        tuple(range(head, min(head + 2, heads))) for head in range(1, heads, 2)
    ]
    project(groups[0])
    for place, group in enumerate(groups):
        if place + 1 < len(groups):
            project(groups[place + 1])
        for head in group:
            attend(head)
        for head in group:
            send(head)

    @pl.when(stage == 0)
    def _():
        for copy in latent_sends_x() + latent_passes():
            copy.wait_send()

    @pl.when(stage == helper)
    def _():
        for copy in latent_sends_y():
            copy.wait_send()

    @pl.when(stage > 0)
    def _():
        back_copy(stage - 1).wait_send()

        def passed(head, carry):
            for copy in next_passes(head):
                copy.wait_send()
            return carry

        lax.fori_loop(0, heads, passed, 0)

    @pl.when(stage < last)
    def _():
        def sent(head, carry):
            for copy in next_sends(head):
                copy.wait_send()
            return carry

        lax.fori_loop(0, heads, sent, 0)
        back_copy(stage + 1).wait_recv()

    @pl.when(stage == last)
    def _():
        def done(head, carry):
            out_own(head).wait()
            for step in range(1, seq_count):
                out_copy(head, step).wait_send()
                out_arrival(head, peer(step)).wait_recv()
            return carry

        lax.fori_loop(0, heads, done, 0)


def local(latent, w_qkv, modulation, timestep, order, tiles, stale_kv):
    patches, rows_dev, width = latent.shape
    local_w = w_qkv.shape[3]
    heads = local_w // HEAD_DIM
    seq_count = lax.axis_size("seq")
    pipe_count = lax.axis_size("pipe")
    block = patches * rows_dev
    tokens = block * seq_count
    weights = jnp.transpose(w_qkv[0], (1, 0, 2))
    stale = stale_kv[0].reshape(tokens, 2, local_w)
    mods = jnp.transpose(modulation[0], (1, 0, 2))
    smem = pl.BlockSpec(memory_space=pltpu.SMEM)
    vmem = pl.BlockSpec(memory_space=pltpu.VMEM)
    anywhere = pl.BlockSpec(memory_space=pl.ANY)
    bf16 = jnp.bfloat16
    dma = pltpu.SemaphoreType.DMA
    finished = pl.pallas_call(
        functools.partial(kernel, (patches, rows_dev, seq_count, pipe_count, heads)),
        out_shape=jax.ShapeDtypeStruct((block, width), bf16),
        in_specs=[smem, smem, anywhere, anywhere, anywhere, vmem, anywhere],
        out_specs=anywhere,
        scratch_shapes=[
            pltpu.VMEM((tokens, width), bf16),
            pltpu.VMEM((seq_count * heads, tokens, HEAD_DIM), bf16),
            pltpu.VMEM((tokens, width), bf16),
            pltpu.VMEM((3, width, local_w), bf16),
            pltpu.VMEM((tokens, 2, local_w), bf16),
            pltpu.VMEM((2 * tokens, local_w), bf16),
            pltpu.VMEM((2, tokens, local_w), bf16),
            pltpu.VMEM((8, width), jnp.float32),
            pltpu.VMEM((2, tokens, tokens), jnp.float32),
            pltpu.VMEM((heads, tokens, HEAD_DIM), bf16),
            pltpu.VMEM((heads, 3, tokens, HEAD_DIM), bf16),
            dma((3,)),
            dma(()),
            dma(()),
            dma((6,)),
            dma((seq_count, 2)),
            dma((heads, 6)),
            dma((heads, seq_count, 2)),
            dma((heads, 2)),
            dma((heads, seq_count)),
            dma((heads, seq_count)),
            dma(()),
            dma(()),
            pltpu.VMEM(mods.shape, jnp.float32),
            dma(()),
        ],
        compiler_params=pltpu.CompilerParams(
            collective_id=0, has_side_effects=True, vmem_limit_bytes=56 * 1024 * 1024
        ),
    )(timestep, order, latent.reshape(block, width), weights, mods, tiles.T, stale)
    return finished.reshape(1, patches, rows_dev, width)


def solution(mesh):
    return jax.shard_map(
        local,
        mesh=mesh,
        in_specs=(
            P("batch", "seq", None),
            P("pipe", None, None, "seq"),
            P("pipe", None, None, None),
            P(),
            P("batch"),
            P("batch", None),
            P("pipe", "batch", None, None, "seq"),
        ),
        out_specs=P("pipe", "batch", "seq", None),
        check_vma=False,
    )
```
